256 devices in a mesh: dp: 32 (over y, x, core), expert: 8 (over z).
Axes of the slice: x: 4, y: 4, z: 8, core: 2. Of those that a mesh axis runs over, the one named last changes fastest.
Arguments:
- tokens: bfloat16 [65536, 2048], P(('dp', 'expert')), may hold values from -24 to 24
- cotangent: bfloat16 [65536, 2048], P(('dp', 'expert')), may hold values from -24 to 24
- routes: int32 [65536, 2], P(('dp', 'expert')), may hold values from 0 to 7, all different within a row; in each aligned block of 256 rows (0 to 255, 256 to 511, ...) at most 96 rows name the same one
- gate_probs: float32 [65536, 2], P(('dp', 'expert')), may hold values from 0.2 to 1
- w_up: bfloat16 [8, 2048, 768], P('expert'), may hold values from -0.125 to 0.125
- w_down: bfloat16 [8, 768, 2048], P('expert'), may hold values from -0.21875 to 0.21875
- decay_rate: float32 [8, 768], P('expert'), may hold values from 0.3 to 0.95
Outputs:
- layer_out: bfloat16 [65536, 2048], P(('dp', 'expert'))
- token_grad: bfloat16 [65536, 2048], P(('dp', 'expert'))
- gate_grad: float32 [65536, 2], P(('dp', 'expert'))
- up_grad: float32 [8, 2048, 768], P('expert', 'dp')
- down_grad: float32 [8, 768, 2048], P('expert', None, 'dp')
The draws below stay inside these ranges and needn't reach their ends.
Inputs may be any that keep to these rules, and one draw needn't show every extreme that they name: `routes`: each token names two different experts; among the 256 rows of one device no expert is named by more than 96 rows, and in every draw some expert is named by exactly 96 rows of some device.
All inputs are finite; a program needn't handle non-finite values.
Results may differ from the reference program's by a relative error of at most 0.015.
Values may be sent and summed in bfloat16 or wider, within the bound.
No kernel may reach another device: no remote copies, remote signals or barrier semaphores. Data moves between devices by JAX's collectives and lax.ppermute only.
A program may use at most 128 MiB of HBM per device.

```python
import math
from functools import partial
import jax
import jax.numpy as jnp
import numpy as np
from jax import lax

D = 2048
FF = 768
STEPS = 4
TOK_DEV = 256
EXPERTS = 8
CAP = 96
TOKENS = 65536


def strengthened(array, key, source, target, shards_of, factor):
    owner, partner = [(jnp.arange(array.shape[dim]) // (array.shape[dim] // shards_of)).reshape([-1 if axis == dim else 1 for axis in range(array.ndim)]) for dim in (source, target)]
    chosen = jax.random.permutation(key, shards_of)[partner]
    strong = (owner == chosen) | (owner == (partner + shards_of // 2) % shards_of)
    return jnp.where(strong, factor * array, array)


def levels(own_key, shape, shards, smallest, largest):
    def one(axis_at, blocks):
        draws = jax.random.uniform(jax.random.fold_in(jax.random.fold_in(own_key, 6), axis_at), (blocks,), jnp.float32, smallest / len(shards), largest / len(shards))
        return jnp.repeat(jnp.exp(draws), shape[axis_at] // blocks).reshape((-1,) + (1,) * (len(shape) - axis_at - 1))

    loudness = one(*shards[0])
    for cut in shards[1:]:
        loudness = loudness * one(*cut)
    return loudness


def deal_out(stream_key, own, number, rows, count, top, limit, skew):
    order = jax.random.permutation(stream_key, count)
    packed, ordinary = load_shares(count, rows * top, limit, skew, True), load_shares(count, rows * top, limit, skew, False)
    places = jnp.arange(count)

    def named(sizes, turn):
        used = int((sizes > 0).sum())
        fixed = max(1, used // 4)
        passed = fixed + (places - fixed + turn * (used - fixed)) % max(1, count - fixed)
        return jnp.zeros((count,), jnp.int32).at[order[jnp.where(places < fixed, places, passed)]].set(jnp.asarray(sizes, jnp.int32))

    sizes = jnp.where(number % 4 == 0, named(packed, number // 4), named(ordinary, number - number // 4 - 1))
    mixed = jax.random.permutation(jax.random.fold_in(own, 3), count)
    source_of, receiver = mixed[0:count // 2 * 2:2], mixed[1:count // 2 * 2:2]
    margin = jnp.minimum(sizes[source_of] - 1, limit - sizes[receiver]) // 2
    margin = jnp.where((source_of == order[0]) | (receiver == order[0]) | (sizes[receiver] == 0), 0, jnp.maximum(margin, 0))
    passed = jax.random.randint(jax.random.fold_in(own, 4), (count // 2,), 0, 1 << 20) % (margin + 1)
    sizes = sizes.at[source_of].add(-passed).at[receiver].add(passed)
    members = jnp.searchsorted(jnp.cumsum(sizes), jnp.arange(rows * top), side="right").astype(jnp.int32)
    listing = members.reshape(top, rows).T
    listing = listing[jax.random.permutation(jax.random.fold_in(own, 1), rows)]
    turn = jax.random.randint(jax.random.fold_in(own, 2), (rows, 1), 0, top)
    return jnp.take_along_axis(listing, (jnp.arange(top)[None, :] + turn) % top, axis=1)


def load_shares(count, total, limit, skew, full):
    portions = [(1 << 20) // math.isqrt(rank ** skew) + 1 for rank in range(1, count + 1)]
    largest = limit if full else min(limit, max(-(-total // count), total * portions[0] // sum(portions)))
    least = 1 if total - largest >= count - 1 else 0
    counts, spare = [largest] + [least] * (count - 1), total - largest - least * (count - 1)
    while spare > 0:
        candidates = [i for i in range(1, count) if counts[i] < largest] or [i for i in range(1, count) if counts[i] < limit]
        whole, remaining = sum([portions[i] for i in candidates]), spare
        for i in candidates:
            more = min(limit - counts[i], max(1, remaining * portions[i] // whole), spare)
            counts[i] = counts[i] + more
            spare = spare - more
    return np.array(counts)


def noise(stream_key, extent, scale, limit, shards=(), kind=jnp.bfloat16):
    drawn = jax.random.normal(stream_key, extent, jnp.float32) * scale
    if len(shards) > 0:
        drawn = levels(stream_key, extent, shards, -0.22, 0.18) * drawn
    return jnp.clip(drawn, min=-limit, max=limit).astype(kind)


def noise_with(key, shape, width, reach, pieces, heavy, kind=jnp.bfloat16):
    array = width * jax.random.normal(key, shape, jnp.float32)
    if pieces:
        array = array * levels(key, shape, pieces, -0.22, 0.18)
    return jnp.clip(strengthened(array, jax.random.fold_in(key, 3), *heavy), -reach, reach).astype(kind)


def setup_inputs(seed: int = 0) -> dict:
    arg_keys = jax.random.split(jax.random.key(seed), 8)
    tokens = noise_with(arg_keys[0], (TOKENS, D), 1.0, 24.0, ((0, 256),), (0, 1, 256, 6.0))
    cotangent = noise_with(arg_keys[1], (TOKENS, D), 1.0, 24.0, ((0, 256),), (0, 1, 256, 6.0))
    routes_keys = jax.random.split(jax.random.fold_in(arg_keys[2], 1), TOKENS // TOK_DEV)
    routes_turns = jax.random.permutation(jax.random.fold_in(arg_keys[2], 3), TOKENS // TOK_DEV)
    routes = jax.vmap(lambda own, number: deal_out(jax.random.fold_in(arg_keys[2], 2), own, number, TOK_DEV, EXPERTS, 2, CAP, 2))(routes_keys, routes_turns).reshape((TOKENS, 2))
    gate_probs = jnp.clip(0.2 + 0.8 * jax.random.uniform(arg_keys[3], (TOKENS, 2), jnp.float32) ** levels(arg_keys[3], (TOKENS, 2), ((0, 256),), -0.2, 0.2), 0.2, 1.0)
    w_up = noise(arg_keys[4], (EXPERTS, D, FF), D ** -0.5, 0.125, ((0, 8),))
    w_down = noise(arg_keys[5], (EXPERTS, FF, D), FF ** -0.5, 0.21875, ((0, 8),))
    decay_rate = jnp.clip(jnp.exp(math.log(0.95) - 1.1526795 * jax.random.uniform(arg_keys[6], (EXPERTS, FF), jnp.float32) ** levels(arg_keys[6], (EXPERTS, FF), ((0, 8),), -0.2, 0.2)), 0.3, 0.95)
    return {"tokens": tokens, "cotangent": cotangent, "routes": routes, "gate_probs": gate_probs, "w_up": w_up, "w_down": w_down, "decay_rate": decay_rate}


sharpness = 4.0

def spike_rate(current, decay_rate):
    potential = jnp.zeros_like(current)
    running = jnp.zeros_like(current)
    for tick_index in range(STEPS):
        potential = decay_rate * potential + current
        spikes = jax.nn.sigmoid(sharpness * (potential - 1.0))
        potential = potential - spikes
        running = running + spikes
    return running / STEPS

def place_slots(route_rows, experts_here, capacity):
    chosen = route_rows.reshape(-1).astype(jnp.int32)
    onehot = (chosen[:, None] == jnp.arange(experts_here, dtype=jnp.int32)[None, :]).astype(jnp.int32)
    rank_table = (jnp.cumsum(onehot, axis=0) - 1).astype(jnp.int32)
    return chosen * capacity + lax.optimization_barrier(jnp.sum(rank_table * onehot, axis=1)).astype(jnp.int32)

def fill_slots(position, slot_count):
    order = jnp.arange(position.shape[0], dtype=jnp.int32)
    slot_owner = jnp.zeros((slot_count,), jnp.int32).at[position].set(order)
    live_slots = jnp.zeros((slot_count,), jnp.int32).at[position].set(1)
    return (slot_owner, live_slots)

def expert_pass(recv_rows, rows_grad, weight_up, weight_down, rates_decay):
    current = jnp.dot(recv_rows, weight_up, preferred_element_type=jnp.float32)
    rates, pullback = jax.vjp(partial(spike_rate, decay_rate=rates_decay), current)
    rates_low = rates.astype(jnp.bfloat16)
    outputs = jnp.dot(rates_low, weight_down, preferred_element_type=jnp.float32).astype(jnp.bfloat16)
    rate_grad = jnp.dot(rows_grad, weight_down.T, preferred_element_type=jnp.float32)
    current_grad = pullback(rate_grad)[0].astype(jnp.bfloat16)
    rows_back = jnp.dot(current_grad, weight_up.T, preferred_element_type=jnp.float32).astype(jnp.bfloat16)
    return (outputs, rows_back, rates_low, current_grad)

def reference(tokens, cotangent, routes, gate_probs, w_up, w_down, decay_rate):
    blocks = TOKENS // TOK_DEV
    slot_count = EXPERTS * CAP
    position = jax.vmap(partial(place_slots, experts_here=EXPERTS, capacity=CAP))(routes.reshape(blocks, TOK_DEV * 2))
    slot_owner, live_slots = jax.vmap(partial(fill_slots, slot_count=slot_count))(position)
    token_blocks = tokens.reshape(blocks, TOK_DEV, D)
    cot_blocks = cotangent.reshape(blocks, TOK_DEV, D)
    gate_blocks = gate_probs.reshape(blocks, TOK_DEV * 2)
    take_rows = jax.vmap(lambda source, index: source[index])

    def one_expert(operands):
        weight_up, weight_down, rates_decay, expert_id = operands
        owners = lax.dynamic_slice_in_dim(slot_owner, expert_id * CAP, CAP, 1)
        live = lax.dynamic_slice_in_dim(live_slots, expert_id * CAP, CAP, 1) > 0
        token_index = owners // 2
        zero = jnp.zeros((), jnp.bfloat16)
        recv_rows = jnp.where(live[:, :, None], take_rows(token_blocks, token_index), zero)
        slot_gates = take_rows(gate_blocks, owners)
        scaled = (slot_gates[:, :, None] * take_rows(cot_blocks, token_index).astype(jnp.float32)).astype(jnp.bfloat16)
        rows_grad = jnp.where(live[:, :, None], scaled, zero)
        flat_rows = recv_rows.reshape(blocks * CAP, D)
        flat_grad = rows_grad.reshape(blocks * CAP, D)
        outputs, rows_back, rates_low, current_grad = expert_pass(flat_rows, flat_grad, weight_up, weight_down, rates_decay)
        grad_up = jnp.dot(flat_rows.T, current_grad, preferred_element_type=jnp.float32)
        grad_down = jnp.dot(rates_low.T, flat_grad, preferred_element_type=jnp.float32)
        return (outputs.reshape(blocks, CAP, D), rows_back.reshape(blocks, CAP, D), grad_up, grad_down)
    expert_ids = jnp.arange(EXPERTS, dtype=jnp.int32)
    expert_out, expert_back, up_grad, down_grad = lax.map(one_expert, (w_up, w_down, decay_rate, expert_ids))
    chosen = routes.reshape(blocks, TOK_DEV * 2).astype(jnp.int32)
    block_ids = jnp.arange(blocks, dtype=jnp.int32)[:, None]
    assign_index = ((chosen * blocks + block_ids) * CAP + (position - chosen * CAP)).reshape(-1)
    flat_out = expert_out.reshape(-1, D)[assign_index].reshape(TOKENS, 2, D).astype(jnp.float32)
    flat_back = expert_back.reshape(-1, D)[assign_index].reshape(TOKENS, 2, D).astype(jnp.float32)
    layer_out = lax.optimization_barrier(jnp.sum(gate_probs[:, :, None] * flat_out, axis=1)).astype(jnp.bfloat16)
    gate_grad = lax.optimization_barrier(jnp.sum(cotangent[:, None, :].astype(jnp.float32) * flat_out, axis=2))
    token_grad = lax.optimization_barrier(jnp.sum(flat_back, axis=1)).astype(jnp.bfloat16)
    return (layer_out, token_grad, gate_grad, up_grad, down_grad)
```

```python
from functools import partial

import jax
import jax.numpy as jnp
from jax import lax
from jax.sharding import PartitionSpec as P

STEPS = 4
SHARPNESS = 4.0
BF = jnp.bfloat16
F32 = jnp.float32


def spike_rate(current, decay_rate):
    potential = jnp.zeros_like(current)
    running = jnp.zeros_like(current)
    for _ in range(STEPS):
        potential = decay_rate * potential + current
        spikes = jax.nn.sigmoid(SHARPNESS * (potential - 1.0))
        potential = potential - spikes
        running = running + spikes
    return running / STEPS


def dot(a, b, ca, cb):
    return lax.dot_general(a, b, (((ca,), (cb,)), ((), ())), preferred_element_type=F32)


def local(tokens, cotangent, routes, gate_probs, w_up, w_down, decay_rate):
    rows, width = tokens.shape
    hidden = w_up.shape[2]
    groups = lax.axis_size("expert")
    data = lax.axis_size("dp")
    half = groups // 2
    cap = 3 * rows // groups
    z = lax.axis_index("expert")
    dp = lax.axis_index("dp")
    first_core = (dp % 2) == 0
    chips = data // 2
    same_core = [list(range(0, data, 2)), list(range(1, data, 2))]

    def over_z(x, step):
        return lax.ppermute(x, "expert", [(i, (i + step) % groups) for i in range(groups)])

    def over_core(x):
        return lax.ppermute(x, "dp", [(i, i ^ 1) for i in range(data)])

    part = width // data
    up_slice = lax.dynamic_slice_in_dim(w_up[0], dp * part, part, 0)
    down_slice = lax.dynamic_slice_in_dim(w_down[0], dp * part, part, 1).T
    slices = over_z(jnp.concatenate([up_slice, down_slice], axis=0), half)
    gathered = lax.all_gather(slices, "dp", axis=0, tiled=False)
    up_far = gathered[:, :part].reshape(width, hidden)
    down_far = gathered[:, part:].reshape(width, hidden)
    decay_far = over_z(decay_rate, half)

    ids = lax.broadcasted_iota(jnp.int32, (groups, 1), 0)
    first = routes[:, 0][None, :] == ids
    second = routes[:, 1][None, :] == ids
    named = first | second
    tri = (
        lax.broadcasted_iota(jnp.int32, (rows, rows), 0)
        < lax.broadcasted_iota(jnp.int32, (rows, rows), 1)
    ).astype(BF)
    rank = jnp.where(named, dot(named.astype(BF), tri, 1, 0), -1.0)
    gates = jnp.where(first, gate_probs[:, 0][None, :], 0.0) + jnp.where(
        second, gate_probs[:, 1][None, :], 0.0
    )
    meta = jnp.concatenate([rank, gates], axis=0)

    meta_m, meta_p = over_z(meta, 1), over_z(meta, -1)
    meta_a, meta_b = over_z(meta, 2), over_z(meta, -2)
    tok_m, tok_p = over_z(tokens, 1), over_z(tokens, -1)
    cot_m, cot_p = over_z(cotangent, 1), over_z(cotangent, -1)

    slot = lax.broadcasted_iota(jnp.int32, (cap, 1), 0).astype(F32)

    def pick(table, offset):
        e = (z + offset) % groups
        hit = lax.dynamic_slice_in_dim(table, e, 1, 0) == slot
        gate = lax.dynamic_slice_in_dim(table, e + groups, 1, 0)
        return hit.astype(BF), hit, jnp.sum(jnp.where(hit, gate, 0.0), axis=1, keepdims=True)

    p0n, p0f = pick(meta, 0), pick(meta, half)
    pmn, pmf, pmx = pick(meta_m, 0), pick(meta_m, half), pick(meta_m, 1)
    ppn, ppf, ppx = pick(meta_p, 0), pick(meta_p, half), pick(meta_p, groups - 1)
    pan, pbn = pick(meta_a, 0), pick(meta_b, 0)

    def take(p, source):
        return dot(p[0], source, 1, 0).astype(BF)

    tok_a = over_z(take(pmx, tok_m), 1)
    tok_b = over_z(take(ppx, tok_p), -1)
    cot_a = over_z(take(pmx, cot_m), 1)
    cot_b = over_z(take(ppx, cot_p), -1)

    near = [p0n, pmn, ppn, pan, pbn]
    far = [p0f, pmf, ppf]
    x_near = jnp.concatenate(
        [take(p0n, tokens), take(pmn, tok_m), take(ppn, tok_p), tok_a, tok_b], axis=0
    )
    x_far = jnp.concatenate([take(p0f, tokens), take(pmf, tok_m), take(ppf, tok_p)], axis=0)
    c_near = jnp.concatenate(
        [take(p0n, cotangent), take(pmn, cot_m), take(ppn, cot_p), cot_a, cot_b], axis=0
    )
    c_far = jnp.concatenate(
        [take(p0f, cotangent), take(pmf, cot_m), take(ppf, cot_p)], axis=0
    )
    g_near = jnp.concatenate([p[2] for p in near], axis=0)
    g_far = jnp.concatenate([p[2] for p in far], axis=0)

    def expert(x, c, gate, up, down, decay, contract):
        current = dot(x, up, 1, 0)
        rates, pullback = jax.vjp(partial(spike_rate, decay_rate=decay), current)
        rates = rates.astype(BF)
        out_grad = (gate * c.astype(F32)).astype(BF)
        rate_grad = dot(out_grad, down, 1, contract)
        current_grad = pullback(rate_grad)[0].astype(BF)
        return rates, out_grad, current_grad

    rates_f, og_f, cg_f = expert(x_far, c_far, g_far, up_far, down_far, decay_far, 0)
    rates_n, og_n, cg_n = expert(x_near, c_near, g_near, w_up[0], w_down[0], decay_rate, 1)

    def weight_grad(x, og, rates, cg):
        wide_keep = jnp.where(first_core, x, og)
        wide_send = jnp.where(first_core, og, x)
        thin_keep = jnp.where(first_core, cg, rates)
        thin_send = jnp.where(first_core, rates, cg)
        wide_got, thin_got = over_core(wide_send), over_core(thin_send)
        total = dot(wide_keep, thin_keep, 0, 0) + dot(wide_got, thin_got, 0, 0)
        parts = total.astype(BF).reshape(chips, width // chips, hidden)
        parts = lax.all_to_all(
            parts, "dp", split_axis=0, concat_axis=0, tiled=True, axis_index_groups=same_core
        )
        return jnp.sum(parts.astype(F32), axis=0)

    sum_far = weight_grad(x_far, og_f, rates_f, cg_f)
    sum_near = weight_grad(x_near, og_n, rates_n, cg_n)
    total = sum_near + over_z(sum_far.astype(BF), half).astype(F32)
    keep = jnp.where(first_core, total[:part], total[part:])
    send = jnp.where(first_core, total[part:], total[:part])
    got = over_core(send)
    up_grad = jnp.where(first_core, keep, got)
    down_grad = jnp.where(first_core, got, keep)

    out_n = dot(rates_n, w_down[0], 1, 0)
    back_n = dot(cg_n, w_up[0], 1, 1).astype(BF)
    out_f = dot(rates_f, down_far, 1, 1)
    back_f = dot(cg_f, up_far, 1, 1).astype(BF)
    inner_n = jnp.sum(out_n * c_near.astype(F32), axis=1, keepdims=True)
    inner_f = jnp.sum(out_f * c_far.astype(F32), axis=1, keepdims=True)
    out_n = (g_near * out_n).astype(BF)
    out_f = (g_far * out_f).astype(BF)

    def block(array, i):
        return array[i * cap : (i + 1) * cap]

    def partial_sums(n, f):
        got_m = over_z(block(n, 3), -1)
        got_p = over_z(block(n, 4), 1)
        sum_m = (
            dot(pmn[0], block(n, 1), 0, 0)
            + dot(pmf[0], block(f, 1), 0, 0)
            + dot(pmx[0], got_m, 0, 0)
        )
        sum_p = (
            dot(ppn[0], block(n, 2), 0, 0)
            + dot(ppf[0], block(f, 2), 0, 0)
            + dot(ppx[0], got_p, 0, 0)
        )
        sum_0 = dot(p0n[0], block(n, 0), 0, 0) + dot(p0f[0], block(f, 0), 0, 0)
        home_a = over_z(sum_m.astype(BF), -1)
        home_b = over_z(sum_p.astype(BF), 1)
        return (sum_0 + home_a.astype(F32) + home_b.astype(F32)).astype(BF)

    layer_out = partial_sums(out_n, out_f)
    token_grad = partial_sums(back_n, back_f)

    def spread(p, inner):
        return jnp.sum(jnp.where(p[1], inner, 0.0), axis=0, keepdims=True)

    gg_0 = jnp.concatenate([spread(p0n, block(inner_n, 0)), spread(p0f, block(inner_f, 0))], 0)
    gg_m = jnp.concatenate([spread(pmn, block(inner_n, 1)), spread(pmf, block(inner_f, 1))], 0)
    gg_p = jnp.concatenate([spread(ppn, block(inner_n, 2)), spread(ppf, block(inner_f, 2))], 0)
    gg_a = spread(pan, block(inner_n, 3))
    gg_b = spread(pbn, block(inner_n, 4))
    from_p, from_m = over_z(gg_m, -1), over_z(gg_p, 1)
    from_b, from_a = over_z(gg_a, -2), over_z(gg_b, 2)
    table = jnp.concatenate(
        [
            gg_0[0:1],
            from_p[0:1],
            from_b,
            from_m[1:2],
            gg_0[1:2],
            from_p[1:2],
            from_a,
            from_m[0:1],
        ],
        axis=0,
    )
    offset = lax.broadcasted_iota(jnp.int32, (groups, 1), 0)

    def gate_of(k):
        hit = ((routes[:, k] - z) % groups)[None, :] == offset
        return jnp.sum(jnp.where(hit, table, 0.0), axis=0)

    gate_grad = jnp.stack([gate_of(0), gate_of(1)], axis=1)
    return (layer_out, token_grad, gate_grad, up_grad[None], down_grad.T[None])


def solution(mesh):
    rows = P(("dp", "expert"), None)
    return jax.shard_map(
        local,
        mesh=mesh,
        in_specs=(rows, rows, rows, rows, P("expert", None, None), P("expert", None, None), P("expert", None)),
        out_specs=(rows, rows, rows, P("expert", "dp", None), P("expert", None, "dp")),
        check_vma=False,
    )
```

```python
from functools import partial

import jax
import jax.numpy as jnp
from jax import lax
from jax.experimental import pallas as pl
from jax.experimental.pallas import tpu as pltpu
from jax.sharding import PartitionSpec as P

STEPS = 4
SHARPNESS = 4.0
BF = jnp.bfloat16
F32 = jnp.float32
VMEM_LIMIT = 56 * 1024 * 1024


def dot(a, b, ca, cb):
    return lax.dot_general(a, b, (((ca,), (cb,)), ((), ())), preferred_element_type=F32)


def call(body, grid, in_specs, out_specs, out_shape, scratch, flops, moved):
    return pl.pallas_call(
        body,
        grid=grid,
        in_specs=in_specs,
        out_specs=out_specs,
        out_shape=out_shape,
        scratch_shapes=scratch,
        compiler_params=pltpu.CompilerParams(
            dimension_semantics=("arbitrary",) * len(grid), vmem_limit_bytes=VMEM_LIMIT
        ),
        cost_estimate=pl.CostEstimate(flops=flops, bytes_accessed=moved, transcendentals=0),
    )


def whole(shape):
    return pl.BlockSpec(shape, lambda j: (0,) * len(shape))


def scalars():
    return pl.BlockSpec(memory_space=pltpu.SMEM)


def rank_row(table, e, groups):
    return table[pl.ds(lax.rem(e, groups), 1), :]


def gate_row(table, e, groups):
    return table[pl.ds(lax.rem(e, groups) + groups, 1), :]


def hits(table, e, groups, cap):
    slot = lax.broadcasted_iota(jnp.int32, (cap, table.shape[1]), 0).astype(F32)
    return rank_row(table, e, groups) == slot


def one_hot(table, e, groups, cap):
    return jnp.where(hits(table, e, groups, cap), 1.0, 0.0).astype(BF)


def pick_kernel(groups, cap, place, t0, tm, tp, x0, xm, xp, kept, on_m, on_p):
    z = place[0]
    half = groups // 2

    def take(table, off, src):
        return dot(one_hot(table, z + off, groups, cap), src[...], 1, 0).astype(BF)

    on_m[...] = take(tm, 1, xm)
    on_p[...] = take(tp, groups - 1, xp)
    for i, (table, src) in enumerate(((t0, x0), (tm, xm), (tp, xp))):
        kept[i * cap : (i + 1) * cap, :] = take(table, 0, src)
        kept[(3 + i) * cap : (4 + i) * cap, :] = take(table, half, src)


def forward_kernel(cap, x, xa, xb, up, up_far, decay, decay_far, rates, slope, near):
    @pl.when(pl.program_id(0) == 0)
    def _():
        near[: 3 * cap, :] = x[: 3 * cap, :]
        near[3 * cap : 4 * cap, :] = xa[...]
        near[4 * cap :, :] = xb[...]

    def neuron(current, leak):
        v = current
        dv = jnp.ones_like(current)
        total = jnp.zeros_like(current)
        grad = jnp.zeros_like(current)
        for step in range(STEPS):
            if step:
                v = leak * v + current
                dv = leak * dv + 1.0
            t = jnp.tanh((0.5 * SHARPNESS) * (v - 1.0))
            spike = 0.5 * t + 0.5
            dspike = (0.25 * SHARPNESS) * (1.0 - t * t) * dv
            v = v - spike
            dv = dv - dspike
            total = total + spike
            grad = grad + dspike
        return total * (1.0 / STEPS), grad * (1.0 / STEPS)

    width = near.shape[1]
    rates[: 5 * cap, :], slope[: 5 * cap, :] = neuron(dot(near[...], up[...], 1, 0), decay[...])
    far = up_far[...].reshape(width, up_far.shape[2])
    rates[5 * cap :, :], slope[5 * cap :, :] = neuron(
        dot(x[3 * cap :, :], far, 1, 0), decay_far[...]
    )


def backward_kernel(
    groups, cap, place, t0, tm, tp, ta, tb, c, ca, cb, down, down_far, rates, slope,
    cg, gated, send, inner, near, gates, products,
):
    z, core = place[0], place[1]
    half = groups // 2
    step = pl.program_id(0)
    pairs = ((t0, 0), (tm, 0), (tp, 0), (ta, 0), (tb, 0), (t0, half), (tm, half), (tp, half))

    @pl.when(step == 0)
    def _():
        near[: 3 * cap, :] = c[: 3 * cap, :]
        near[3 * cap : 4 * cap, :] = ca[...]
        near[4 * cap :, :] = cb[...]
        products[...] = jnp.zeros_like(products)
        for i, (table, off) in enumerate(pairs):
            row = jnp.where(
                hits(table, z + off, groups, cap), gate_row(table, z + off, groups), 0.0
            )
            gates[i * cap : (i + 1) * cap, :] = jnp.broadcast_to(
                jnp.sum(row, axis=1, keepdims=True), (cap, 128)
            )

    far = down_far[...].reshape(near.shape[1], down_far.shape[2])
    for lo, hi, grad in (
        (0, 5 * cap, dot(near[...], down[...], 1, 1)),
        (5 * cap, 8 * cap, dot(c[3 * cap :, :], far, 1, 0)),
    ):
        r = rates[lo:hi, :]
        gate = gates[lo:hi, 0:1]
        both = r * grad
        acc = both[:, :128]
        for k in range(1, both.shape[1] // 128):
            acc = acc + both[:, k * 128 : (k + 1) * 128]
        products[lo:hi, :] += acc
        current = (gate * grad * slope[lo:hi, :]).astype(BF)
        scaled = (gate * r).astype(BF)
        cg[lo:hi, :] = current
        gated[lo:hi, :] = scaled
        send[lo:hi, :] = jnp.where(core == 0, scaled, current)

    @pl.when(step == pl.num_programs(0) - 1)
    def _():
        for i, (table, off) in enumerate(pairs):
            value = jnp.sum(products[i * cap : (i + 1) * cap, :], axis=1, keepdims=True)
            inner[i : i + 1, :] = jnp.sum(
                jnp.where(hits(table, z + off, groups, cap), value, 0.0), axis=0, keepdims=True
            )


def weight_kernel(
    cap, place, x, xa, xb, c, ca, cb, got, got_a, got_b, cg, gated, got_thin, out,
    wide_n, wide_f, thin_n, thin_f,
):
    first = place[1] == 0
    three, five = 3 * cap, 5 * cap

    def own(a, b):
        return jnp.where(first, a, b)

    @pl.when(pl.program_id(0) == 0)
    def _():
        thin_n[:five, :] = own(cg[:five, :], gated[:five, :])
        thin_n[five:, :] = got_thin[:five, :]
        thin_f[:three, :] = own(cg[five:, :], gated[five:, :])
        thin_f[three:, :] = got_thin[five:, :]

    wide_n[:three, :] = own(x[:three, :], c[:three, :])
    wide_n[three : 4 * cap, :] = own(xa[...], ca[...])
    wide_n[4 * cap : five, :] = own(xb[...], cb[...])
    wide_n[five : five + three, :] = got[:three, :]
    wide_n[five + three : five + 4 * cap, :] = got_a[...]
    wide_n[five + 4 * cap :, :] = got_b[...]
    wide_f[:three, :] = own(x[three:, :], c[three:, :])
    wide_f[three:, :] = got[three:, :]
    chips, both, hidden = out.shape
    each = both // 2
    near = dot(wide_n[...], thin_n[...], 0, 0).astype(BF)
    far = dot(wide_f[...], thin_f[...], 0, 0).astype(BF)
    out[:, :each, :] = near.reshape(chips, each, hidden)
    out[:, each:, :] = far.reshape(chips, each, hidden)


def onward_kernel(cap, cg, gated, up, down, out_a, out_b, back_a, back_b):
    out = dot(gated[3 * cap : 5 * cap, :], down[...], 1, 0).astype(BF)
    back = dot(cg[3 * cap : 5 * cap, :], up[...], 1, 1).astype(BF)
    out_a[...], out_b[...] = out[:cap], out[cap:]
    back_a[...], back_b[...] = back[:cap], back[cap:]


def rows_kernel(cap, cg, gated, up, down, up_far, down_far, out, back):
    hidden = up.shape[1]
    three, five = 3 * cap, 5 * cap
    uf = up_far[...].reshape(up.shape[0], hidden)
    df = down_far[...].reshape(up.shape[0], hidden)
    out[:three, :] = dot(gated[:three, :], down[...], 1, 0).astype(BF)
    out[three:, :] = dot(gated[five:, :], df, 1, 1).astype(BF)
    back[:three, :] = dot(cg[:three, :], up[...], 1, 1).astype(BF)
    back[three:, :] = dot(cg[five:, :], uf, 1, 1).astype(BF)


def return_kernel(groups, cap, place, tm, tp, rows, got_m, got_p, to_m, to_p):
    z = place[0]
    half = groups // 2

    def put(table, off, values):
        return dot(one_hot(table, z + off, groups, cap), values, 0, 0)

    for table, i, extra, got, to in (
        (tm, 1, 1, got_m, to_m),
        (tp, 2, groups - 1, got_p, to_p),
    ):
        total = put(table, 0, rows[i * cap : (i + 1) * cap, :])
        total += put(table, half, rows[(3 + i) * cap : (4 + i) * cap, :])
        total += put(table, extra, got[...])
        to[...] = total.astype(BF)


def final_kernel(groups, cap, place, t0, rows, a, b, result):
    z = place[0]
    half = groups // 2
    total = dot(one_hot(t0, z, groups, cap), rows[:cap, :], 0, 0)
    total += dot(one_hot(t0, z + half, groups, cap), rows[3 * cap : 4 * cap, :], 0, 0)
    total += a[...].astype(F32) + b[...].astype(F32)
    result[...] = total.astype(BF)


def local(tokens, cotangent, routes, gate_probs, w_up, w_down, decay_rate):
    rows, width = tokens.shape
    hidden = w_up.shape[2]
    groups = lax.axis_size("expert")
    data = lax.axis_size("dp")
    half = groups // 2
    cap = 3 * rows // groups
    z = lax.axis_index("expert")
    dp = lax.axis_index("dp")
    core = dp % 2
    first_core = core == 0
    chips = data // 2
    same_core = [list(range(0, data, 2)), list(range(1, data, 2))]
    place = jnp.stack([z, core]).astype(jnp.int32)
    up, down = w_up[0], w_down[0]

    def over_z(x, step):
        return lax.ppermute(x, "expert", [(i, (i + step) % groups) for i in range(groups)])

    def over_core(x):
        return lax.ppermute(x, "dp", [(i, i ^ 1) for i in range(data)])

    def after(x, *done):
        return lax.optimization_barrier((x, *done))[0]

    part = width // data
    up_slice = lax.dynamic_slice_in_dim(up, dp * part, part, 0)
    down_slice = lax.dynamic_slice_in_dim(down, dp * part, part, 1).T
    slices = over_z(jnp.concatenate([up_slice, down_slice], axis=0), half)
    gathered = lax.all_gather(slices, "dp", axis=0, tiled=False)
    decay_far = over_z(decay_rate, half)

    ids = lax.broadcasted_iota(jnp.int32, (groups, 1), 0)
    first = routes[:, 0][None, :] == ids
    second = routes[:, 1][None, :] == ids
    named = first | second
    tri = (
        lax.broadcasted_iota(jnp.int32, (rows, rows), 0)
        < lax.broadcasted_iota(jnp.int32, (rows, rows), 1)
    ).astype(BF)
    rank = jnp.where(named, dot(named.astype(BF), tri, 1, 0), -1.0)
    gates = jnp.where(first, gate_probs[:, 0][None, :], 0.0) + jnp.where(
        second, gate_probs[:, 1][None, :], 0.0
    )
    t0 = jnp.concatenate([rank, gates], axis=0)
    tm, tp, ta, tb = over_z(t0, 1), over_z(t0, -1), over_z(t0, 2), over_z(t0, -2)

    tokens = after(tokens, slices, tm, tp, ta, tb, decay_far)
    tok_m, tok_p = over_z(tokens, 1), over_z(tokens, -1)
    cotangent = after(cotangent, tok_m, tok_p)
    cot_m, cot_p = over_z(cotangent, 1), over_z(cotangent, -1)

    mb = 1 << 20
    table_spec = whole((2 * groups, rows))
    tile = 512
    steps = width // tile

    def cols(n):
        return pl.BlockSpec((n, tile), lambda j: (0, j))

    picks = call(
        partial(pick_kernel, groups, cap),
        (steps,),
        [scalars()] + [table_spec] * 3 + [cols(rows)] * 3,
        [cols(6 * cap), cols(cap), cols(cap)],
        [
            jax.ShapeDtypeStruct((6 * cap, width), BF),
            jax.ShapeDtypeStruct((cap, width), BF),
            jax.ShapeDtypeStruct((cap, width), BF),
        ],
        [],
        2 * 8 * cap * rows * width,
        6 * mb,
    )
    x, x_on_m, x_on_p = picks(place, t0, tm, tp, tokens, tok_m, tok_p)
    xa, xb = over_z(x_on_m, 1), over_z(x_on_p, -1)
    c, c_on_m, c_on_p = picks(place, t0, tm, tp, cotangent, cot_m, cot_p)
    ca, cb = over_z(c_on_m, 1), over_z(c_on_p, -1)

    ff = 256
    ff_steps = hidden // ff

    def ff_cols(n):
        return pl.BlockSpec((n, ff), lambda j: (0, j))

    def far_ff(which):
        return pl.BlockSpec((data, part, ff), lambda j: (0, which, j))

    total = 8 * cap
    rates, slope = call(
        partial(forward_kernel, cap),
        (ff_steps,),
        [
            whole((6 * cap, width)), whole((cap, width)), whole((cap, width)),
            ff_cols(width), far_ff(0), ff_cols(1), ff_cols(1),
        ],
        [ff_cols(total)] * 2,
        [jax.ShapeDtypeStruct((total, hidden), F32)] * 2,
        [pltpu.VMEM((5 * cap, width), BF)],
        2 * total * width * hidden,
        16 * mb,
    )(x, xa, xb, up, gathered, decay_rate, decay_far)

    cg, gated, send, inner = call(
        partial(backward_kernel, groups, cap),
        (ff_steps,),
        [scalars()] + [table_spec] * 5
        + [
            whole((6 * cap, width)), whole((cap, width)), whole((cap, width)),
            pl.BlockSpec((ff, width), lambda j: (j, 0)), far_ff(1), ff_cols(total), ff_cols(total),
        ],
        [ff_cols(total)] * 3 + [whole((groups, rows))],
        [jax.ShapeDtypeStruct((total, hidden), BF)] * 3
        + [jax.ShapeDtypeStruct((groups, rows), F32)],
        [
            pltpu.VMEM((5 * cap, width), BF),
            pltpu.VMEM((total, 128), F32),
            pltpu.VMEM((total, 128), F32),
        ],
        2 * total * width * hidden,
        18 * mb,
    )(place, t0, tm, tp, ta, tb, c, ca, cb, down, gathered, rates, slope)

    got = over_core(jnp.where(first_core, c, x))
    got_a = over_core(jnp.where(first_core, ca, xa))
    got_b = over_core(jnp.where(first_core, cb, xb))
    got_thin = over_core(send)
    pair = 2
    span = pair * width // chips

    def span_cols(n):
        return pl.BlockSpec((n, span), lambda j: (0, j))

    wide = [span_cols(6 * cap), span_cols(cap), span_cols(cap)]
    parts = call(
        partial(weight_kernel, cap),
        (chips // pair,),
        [scalars()] + wide * 3 + [whole((total, hidden))] * 3,
        pl.BlockSpec((pair, 2 * width // chips, hidden), lambda j: (j, 0, 0)),
        jax.ShapeDtypeStruct((chips, 2 * width // chips, hidden), BF),
        [
            pltpu.VMEM((10 * cap, span), BF),
            pltpu.VMEM((6 * cap, span), BF),
            pltpu.VMEM((10 * cap, hidden), BF),
            pltpu.VMEM((6 * cap, hidden), BF),
        ],
        4 * total * width * hidden,
        20 * mb,
    )(place, x, xa, xb, c, ca, cb, got, got_a, got_b, cg, gated, got_thin)
    parts = lax.all_to_all(
        parts, "dp", split_axis=0, concat_axis=0, tiled=True, axis_index_groups=same_core
    )
    sums = jnp.sum(parts.astype(F32), axis=0)
    each = width // chips
    weight = sums[:each] + over_z(sums[each:].astype(BF), half).astype(F32)
    keep = jnp.where(first_core, weight[:part], weight[part:])
    give = jnp.where(first_core, weight[part:], weight[:part])
    other = over_core(give)
    up_grad = jnp.where(first_core, keep, other)
    down_grad = jnp.where(first_core, other, keep)

    up_rows = pl.BlockSpec((tile, hidden), lambda j: (j, 0))
    row_shape = jax.ShapeDtypeStruct((cap, width), BF)
    out_a, out_b, back_a, back_b = call(
        partial(onward_kernel, cap),
        (steps,),
        [whole((total, hidden))] * 2 + [up_rows, cols(hidden)],
        [cols(cap)] * 4,
        [row_shape] * 4,
        [],
        8 * cap * width * hidden,
        9 * mb,
    )(cg, gated, up, down)
    out_got_m, out_got_p = over_z(out_a, -1), over_z(out_b, 1)
    back_got_m, back_got_p = over_z(back_a, -1), over_z(back_b, 1)

    def far_rows(which):
        return pl.BlockSpec((tile // part, part, hidden), lambda j: (j, which, 0))

    out, back = call(
        partial(rows_kernel, cap),
        (steps,),
        [whole((total, hidden))] * 2 + [up_rows, cols(hidden), far_rows(0), far_rows(1)],
        [cols(6 * cap)] * 2,
        [jax.ShapeDtypeStruct((6 * cap, width), BF)] * 2,
        [],
        24 * cap * width * hidden,
        18 * mb,
    )(cg, gated, up, down, gathered, gathered)

    block = jax.ShapeDtypeStruct((rows, width), BF)
    returns = call(
        partial(return_kernel, groups, cap),
        (steps,),
        [scalars()] + [table_spec] * 2 + [cols(6 * cap), cols(cap), cols(cap)],
        [cols(rows)] * 2,
        [block] * 2,
        [],
        12 * cap * rows * width,
        5 * mb,
    )
    finals = call(
        partial(final_kernel, groups, cap),
        (steps,),
        [scalars(), table_spec, cols(6 * cap), cols(rows), cols(rows)],
        cols(rows),
        block,
        [],
        4 * cap * rows * width,
        5 * mb,
    )
    out_m, out_p = returns(place, tm, tp, out, out_got_m, out_got_p)
    layer_out = finals(place, t0, out, over_z(out_m, -1), over_z(out_p, 1))
    back_m, back_p = returns(place, tm, tp, back, back_got_m, back_got_p)
    token_grad = finals(place, t0, back, over_z(back_m, -1), over_z(back_p, 1))

    from_p, from_m = over_z(inner, -1), over_z(inner, 1)
    from_b, from_a = over_z(inner, -2), over_z(inner, 2)
    table = jnp.stack(
        [inner[0], from_p[1], from_b[3], from_m[7], inner[5], from_p[6], from_a[4], from_m[2]]
    )
    offset = lax.broadcasted_iota(jnp.int32, (groups, 1), 0)

    def gate_of(k):
        hit = ((routes[:, k] - z) % groups)[None, :] == offset
        return jnp.sum(jnp.where(hit, table, 0.0), axis=0)

    gate_grad = jnp.stack([gate_of(0), gate_of(1)], axis=1)
    return (layer_out, token_grad, gate_grad, up_grad[None], down_grad.T[None])


def solution(mesh):
    rows = P(("dp", "expert"), None)
    weights = P("expert", None, None)
    return jax.shard_map(
        local,
        mesh=mesh,
        in_specs=(rows, rows, rows, rows, weights, weights, P("expert", None)),
        out_specs=(rows, rows, rows, P("expert", "dp", None), P("expert", None, "dp")),
        check_vma=False,
    )
```

```python
from functools import partial

import jax
import jax.numpy as jnp
from jax import lax
from jax.experimental import pallas as pl
from jax.experimental.pallas import tpu as pltpu
from jax.sharding import PartitionSpec as P

STEPS = 4
SHARPNESS = 4.0
BF = jnp.bfloat16
F32 = jnp.float32
VMEM_LIMIT = 56 * 1024 * 1024


def dot(a, b, ca, cb):
    return lax.dot_general(a, b, (((ca,), (cb,)), ((), ())), preferred_element_type=F32)


def call(body, grid, in_specs, out_specs, out_shape, scratch):
    return pl.pallas_call(
        body,
        grid=grid,
        in_specs=in_specs,
        out_specs=out_specs,
        out_shape=out_shape,
        scratch_shapes=scratch,
        compiler_params=pltpu.CompilerParams(
            dimension_semantics=("arbitrary",) * len(grid), vmem_limit_bytes=VMEM_LIMIT
        ),
        cost_estimate=pl.CostEstimate(flops=0, bytes_accessed=1 << 16, transcendentals=0),
    )


def whole(shape):
    return pl.BlockSpec(shape, lambda j: (0,) * len(shape))


def scalars():
    return pl.BlockSpec(memory_space=pltpu.SMEM)


def rank_row(table, e, groups):
    return table[pl.ds(lax.rem(e, groups), 1), :]


def gate_row(table, e, groups):
    return table[pl.ds(lax.rem(e, groups) + groups, 1), :]


def hits(table, e, groups, cap):
    slot = lax.broadcasted_iota(jnp.int32, (cap, table.shape[1]), 0).astype(F32)
    return rank_row(table, e, groups) == slot


def one_hot(table, e, groups, cap):
    return jnp.where(hits(table, e, groups, cap), 1.0, 0.0).astype(BF)


def pick_kernel(groups, cap, place, t0, tm, tp, x0, xm, xp, kept, on_m, on_p):
    z = place[0]
    half = groups // 2

    def take(table, off, src):
        return dot(one_hot(table, z + off, groups, cap), src[...], 1, 0).astype(BF)

    on_m[...] = take(tm, 1, xm)
    on_p[...] = take(tp, groups - 1, xp)
    for i, (table, src) in enumerate(((t0, x0), (tm, xm), (tp, xp))):
        kept[i * cap : (i + 1) * cap, :] = take(table, 0, src)
        kept[(3 + i) * cap : (4 + i) * cap, :] = take(table, half, src)


def neuron(current, leak):
    v = current
    dv = jnp.ones_like(current)
    total = jnp.zeros_like(current)
    grad = jnp.zeros_like(current)
    for step in range(STEPS):
        if step:
            v = leak * v + current
            dv = leak * dv + 1.0
        t = jnp.tanh((0.5 * SHARPNESS) * (v - 1.0))
        spike = 0.5 * t + 0.5
        dspike = (0.25 * SHARPNESS) * (1.0 - t * t) * dv
        v = v - spike
        dv = dv - dspike
        total = total + spike
        grad = grad + dspike
    return total * (1.0 / STEPS), grad * (1.0 / STEPS)


def near_kernel(cap, x, xa, xb, up, decay, rates, slope, near):
    @pl.when(pl.program_id(0) == 0)
    def _():
        near[: 3 * cap, :] = x[...]
        near[3 * cap : 4 * cap, :] = xa[...]
        near[4 * cap :, :] = xb[...]

    rates[...], slope[...] = neuron(dot(near[...], up[...], 1, 0), decay[...])


def far_kernel(x, up, decay, rates, slope):
    weights = up[...].reshape(x.shape[1], up.shape[2])
    rates[...], slope[...] = neuron(dot(x[...], weights, 1, 0), decay[...])


def backward_kernel(
    groups, cap, place, t0, tm, tp, ta, tb, c, ca, cb, down, down_far, rates_n, slope_n, rates_f, slope_f,
    cg, gated, send, inner, near, gates, products,
):
    z, core = place[0], place[1]
    half = groups // 2
    step = pl.program_id(0)
    pairs = ((t0, 0), (tm, 0), (tp, 0), (ta, 0), (tb, 0), (t0, half), (tm, half), (tp, half))

    @pl.when(step == 0)
    def _():
        near[: 3 * cap, :] = c[: 3 * cap, :]
        near[3 * cap : 4 * cap, :] = ca[...]
        near[4 * cap :, :] = cb[...]
        products[...] = jnp.zeros_like(products)
        for i, (table, off) in enumerate(pairs):
            row = jnp.where(
                hits(table, z + off, groups, cap), gate_row(table, z + off, groups), 0.0
            )
            gates[i * cap : (i + 1) * cap, :] = jnp.broadcast_to(
                jnp.sum(row, axis=1, keepdims=True), (cap, 128)
            )

    far = down_far[...].reshape(near.shape[1], down_far.shape[2])
    for lo, hi, rates, slope, grad in (
        (0, 5 * cap, rates_n, slope_n, dot(near[...], down[...], 1, 1)),
        (5 * cap, 8 * cap, rates_f, slope_f, dot(c[3 * cap :, :], far, 1, 0)),
    ):
        r = rates[...]
        gate = gates[lo:hi, 0:1]
        both = r * grad
        acc = both[:, :128]
        for k in range(1, both.shape[1] // 128):
            acc = acc + both[:, k * 128 : (k + 1) * 128]
        products[lo:hi, :] += acc
        current = (gate * grad * slope[...]).astype(BF)
        scaled = (gate * r).astype(BF)
        cg[lo:hi, :] = current
        gated[lo:hi, :] = scaled
        send[lo:hi, :] = jnp.where(core == 0, scaled, current)

    @pl.when(step == pl.num_programs(0) - 1)
    def _():
        for i, (table, off) in enumerate(pairs):
            value = jnp.sum(products[i * cap : (i + 1) * cap, :], axis=1, keepdims=True)
            inner[i : i + 1, :] = jnp.sum(
                jnp.where(hits(table, z + off, groups, cap), value, 0.0), axis=0, keepdims=True
            )


def lay_out(x_first, grid_width, where, grads, o0, o1, o2a, o2b, o3):
    step = pl.program_id(0)
    each = o0.shape[1]
    for k in range(2):
        chip = 2 * step + k
        y, x = chip // grid_width, lax.rem(chip, grid_width)
        main, other = (x, y) if x_first else (y, x)
        away = lax.rem(main - where + grid_width, grid_width)
        value = grads[k * each : (k + 1) * each]
        middle = grid_width // 2
        for distance, target in ((0, o0), (1, o1), (3, o3)):

            @pl.when(away == distance)
            def _(target=target, value=value, other=other):
                target[other] = value

        @pl.when((away == 2) & (other < middle))
        def _(value=value, other=other):
            o2a[other] = value

        @pl.when((away == 2) & (other >= middle))
        def _(value=value, other=other):
            o2b[other - middle] = value


def weight_near_kernel(
    cap, side, place, x, xa, xb, c, ca, cb, got, got_a, got_b, cg, gated, got_thin,
    o0, o1, o2a, o2b, o3, wide, thin,
):
    first = place[1] == 0
    three, five = 3 * cap, 5 * cap

    @pl.when(pl.program_id(0) == 0)
    def _():
        thin[:five, :] = jnp.where(first, cg[...], gated[...])
        thin[five:, :] = got_thin[...]

    wide[:three, :] = jnp.where(first, x[...], c[...])
    wide[three : 4 * cap, :] = jnp.where(first, xa[...], ca[...])
    wide[4 * cap : five, :] = jnp.where(first, xb[...], cb[...])
    wide[five : five + three, :] = got[...]
    wide[five + three : five + 4 * cap, :] = got_a[...]
    wide[five + 4 * cap :, :] = got_b[...]
    grads = dot(wide[...], thin[...], 0, 0).astype(BF)
    lay_out(False, side, place[2], grads, o0, o1, o2a, o2b, o3)


def weight_far_kernel(
    cap, side, place, x, c, got, cg, gated, got_thin, o0, o1, o2a, o2b, o3, wide, thin
):
    first = place[1] == 0
    three, five = 3 * cap, 5 * cap

    @pl.when(pl.program_id(0) == 0)
    def _():
        thin[:three, :] = jnp.where(first, cg[five:, :], gated[five:, :])
        thin[three:, :] = got_thin[five:, :]

    wide[:three, :] = jnp.where(first, x[...], c[...])
    wide[three:, :] = got[...]
    grads = dot(wide[...], thin[...], 0, 0).astype(BF)
    lay_out(True, side, place[3], grads, o0, o1, o2a, o2b, o3)


def onward_kernel(cap, cg, gated, up, down, out_a, out_b, back_a, back_b):
    out = dot(gated[3 * cap : 5 * cap, :], down[...], 1, 0).astype(BF)
    back = dot(cg[3 * cap : 5 * cap, :], up[...], 1, 1).astype(BF)
    out_a[...], out_b[...] = out[:cap], out[cap:]
    back_a[...], back_b[...] = back[:cap], back[cap:]


def rows_kernel(cap, cg, gated, up, down, up_far, down_far, out, back):
    hidden = up.shape[1]
    three, five = 3 * cap, 5 * cap
    uf = up_far[...].reshape(up.shape[0], hidden)
    df = down_far[...].reshape(up.shape[0], hidden)
    out[:three, :] = dot(gated[:three, :], down[...], 1, 0).astype(BF)
    out[three:, :] = dot(gated[five:, :], df, 1, 1).astype(BF)
    back[:three, :] = dot(cg[:three, :], up[...], 1, 1).astype(BF)
    back[three:, :] = dot(cg[five:, :], uf, 1, 1).astype(BF)


def return_kernel(groups, cap, place, tm, tp, rows, got_m, got_p, to_m, to_p):
    z = place[0]
    half = groups // 2

    def put(table, off, values):
        return dot(one_hot(table, z + off, groups, cap), values, 0, 0)

    for table, i, extra, got, to in (
        (tm, 1, 1, got_m, to_m),
        (tp, 2, groups - 1, got_p, to_p),
    ):
        total = put(table, 0, rows[i * cap : (i + 1) * cap, :])
        total += put(table, half, rows[(3 + i) * cap : (4 + i) * cap, :])
        total += put(table, extra, got[...])
        to[...] = total.astype(BF)


def final_kernel(groups, cap, place, t0, rows, a, b, result):
    z = place[0]
    half = groups // 2
    total = dot(one_hot(t0, z, groups, cap), rows[:cap, :], 0, 0)
    total += dot(one_hot(t0, z + half, groups, cap), rows[3 * cap : 4 * cap, :], 0, 0)
    total += a[...].astype(F32) + b[...].astype(F32)
    result[...] = total.astype(BF)


def local(tokens, cotangent, routes, gate_probs, w_up, w_down, decay_rate):
    rows, width = tokens.shape
    hidden = w_up.shape[2]
    groups = lax.axis_size("expert")
    data = lax.axis_size("dp")
    half = groups // 2
    cap = 3 * rows // groups
    z = lax.axis_index("expert")
    dp = lax.axis_index("dp")
    core = dp % 2
    first_core = core == 0
    chips = data // 2
    side = 4
    row, col = dp // (2 * side), (dp // 2) % side
    place = jnp.stack([z, core, row, col]).astype(jnp.int32)
    up, down = w_up[0], w_down[0]

    def over_z(x, step):
        return lax.ppermute(x, "expert", [(i, (i + step) % groups) for i in range(groups)])

    def over_core(x):
        return lax.ppermute(x, "dp", [(i, i ^ 1) for i in range(data)])

    def over_x(x, step):
        return lax.ppermute(
            x,
            "dp",
            [(i, i - 2 * (i // 2 % side) + 2 * ((i // 2 + step) % side)) for i in range(data)],
        )

    def over_y(x, step):
        return lax.ppermute(
            x, "dp", [(i, (i + 2 * side * step) % data) for i in range(data)]
        )

    def after(x, *done):
        return lax.optimization_barrier((x, *done))[0]

    part = width // data
    up_slice = lax.dynamic_slice_in_dim(up, dp * part, part, 0)
    down_slice = lax.dynamic_slice_in_dim(down, dp * part, part, 1).T
    slices = over_z(jnp.concatenate([up_slice, down_slice], axis=0), half)
    gathered = lax.all_gather(slices, "dp", axis=0, tiled=False)
    decay_far = over_z(decay_rate, half)

    ids = lax.broadcasted_iota(jnp.int32, (groups, 1), 0)
    first = routes[:, 0][None, :] == ids
    second = routes[:, 1][None, :] == ids
    named = first | second
    tri = (
        lax.broadcasted_iota(jnp.int32, (rows, rows), 0)
        < lax.broadcasted_iota(jnp.int32, (rows, rows), 1)
    ).astype(BF)
    rank = jnp.where(named, dot(named.astype(BF), tri, 1, 0), -1.0)
    gates = jnp.where(first, gate_probs[:, 0][None, :], 0.0) + jnp.where(
        second, gate_probs[:, 1][None, :], 0.0
    )
    t0 = jnp.concatenate([rank, gates], axis=0)
    tm, tp, ta, tb = over_z(t0, 1), over_z(t0, -1), over_z(t0, 2), over_z(t0, -2)

    tokens = after(tokens, slices)
    tok_m, tok_p = over_z(tokens, 1), over_z(tokens, -1)
    cotangent = after(cotangent, tok_m, tok_p, tm, tp)
    cot_m, cot_p = over_z(cotangent, 1), over_z(cotangent, -1)

    table_spec = whole((2 * groups, rows))
    tile = 512
    steps = width // tile

    def cols(n):
        return pl.BlockSpec((n, tile), lambda j: (0, j))

    picks = call(
        partial(pick_kernel, groups, cap),
        (steps,),
        [scalars()] + [table_spec] * 3 + [cols(rows)] * 3,
        [cols(6 * cap), cols(cap), cols(cap)],
        [
            jax.ShapeDtypeStruct((6 * cap, width), BF),
            jax.ShapeDtypeStruct((cap, width), BF),
            jax.ShapeDtypeStruct((cap, width), BF),
        ],
        [],
    )
    x, x_on_m, x_on_p = picks(place, t0, tm, tp, tokens, tok_m, tok_p)
    xa, xb = over_z(x_on_m, 1), over_z(x_on_p, -1)
    c, c_on_m, c_on_p = picks(after(place, xa, xb, ta, tb, decay_far), t0, tm, tp, cotangent, cot_m, cot_p)
    ca, cb = over_z(c_on_m, 1), over_z(c_on_p, -1)

    ff = 256
    ff_steps = hidden // ff

    def ff_cols(n):
        return pl.BlockSpec((n, ff), lambda j: (0, j))

    def far_ff(which):
        return pl.BlockSpec((data, part, ff), lambda j: (0, which, j))

    total = 8 * cap

    def half_rows(i):
        return pl.BlockSpec((3 * cap, width), lambda j: (i, 0))

    rates_n, slope_n = call(
        partial(near_kernel, cap),
        (ff_steps,),
        [half_rows(0), whole((cap, width)), whole((cap, width)), ff_cols(width), ff_cols(1)],
        [ff_cols(5 * cap)] * 2,
        [jax.ShapeDtypeStruct((5 * cap, hidden), F32)] * 2,
        [pltpu.VMEM((5 * cap, width), BF)],
    )(x, xa, xb, up, decay_rate)
    rates_f, slope_f = call(
        far_kernel,
        (ff_steps,),
        [half_rows(1), far_ff(0), ff_cols(1)],
        [ff_cols(3 * cap)] * 2,
        [jax.ShapeDtypeStruct((3 * cap, hidden), F32)] * 2,
        [],
    )(after(x, c, rates_n, ca, cb), gathered, decay_far)

    cg, gated, send, inner = call(
        partial(backward_kernel, groups, cap),
        (ff_steps,),
        [scalars()] + [table_spec] * 5
        + [
            whole((6 * cap, width)), whole((cap, width)), whole((cap, width)),
            pl.BlockSpec((ff, width), lambda j: (j, 0)), far_ff(1),
            ff_cols(5 * cap), ff_cols(5 * cap), ff_cols(3 * cap), ff_cols(3 * cap),
        ],
        [ff_cols(total)] * 3 + [whole((groups, rows))],
        [jax.ShapeDtypeStruct((total, hidden), BF)] * 3
        + [jax.ShapeDtypeStruct((groups, rows), F32)],
        [
            pltpu.VMEM((5 * cap, width), BF),
            pltpu.VMEM((total, 128), F32),
            pltpu.VMEM((total, 128), F32),
        ],
    )(place, t0, tm, tp, ta, tb, c, ca, cb, down, gathered, rates_n, slope_n, rates_f, slope_f)

    got = over_core(jnp.where(first_core, after(c, cg), x))
    got_a = over_core(jnp.where(first_core, ca, xa))
    got_b = over_core(jnp.where(first_core, cb, xb))
    got_thin = over_core(send)
    up_rows = pl.BlockSpec((tile, hidden), lambda j: (j, 0))
    row_shape = jax.ShapeDtypeStruct((cap, width), BF)
    out_a, out_b, back_a, back_b = call(
        partial(onward_kernel, cap),
        (steps,),
        [whole((total, hidden))] * 2 + [up_rows, cols(hidden)],
        [cols(cap)] * 4,
        [row_shape] * 4,
        [],
    )(cg, gated, up, down)
    out_got_m, out_got_p = over_z(out_a, -1), over_z(out_b, 1)
    back_got_m, back_got_p = over_z(back_a, -1), over_z(back_b, 1)

    span = 2 * width // chips

    def span_cols(n, i=0):
        return pl.BlockSpec((n, span), lambda j: (i, j))

    def thin_rows(n):
        return pl.BlockSpec((n, hidden), lambda j: (0, 0))

    each = width // chips
    counts = (side, side, side // 2, side // 2, side)
    laid = [whole((n, each, hidden)) for n in counts]
    laid_shapes = [jax.ShapeDtypeStruct((n, each, hidden), BF) for n in counts]
    far_parts = call(
        partial(weight_far_kernel, cap, side),
        (chips // 2,),
        [scalars()] + [span_cols(3 * cap, 1)] * 3 + [thin_rows(total)] * 3,
        laid,
        laid_shapes,
        [pltpu.VMEM((6 * cap, span), BF), pltpu.VMEM((6 * cap, hidden), BF)],
    )(after(place, out_a), x, c, got, cg, gated, got_thin)
    wide = [span_cols(3 * cap), span_cols(cap), span_cols(cap)]
    near_parts = call(
        partial(weight_near_kernel, cap, side),
        (chips // 2,),
        [scalars()] + wide * 3 + [thin_rows(5 * cap)] * 3,
        laid,
        laid_shapes,
        [pltpu.VMEM((10 * cap, span), BF), pltpu.VMEM((10 * cap, hidden), BF)],
    )(after(place, far_parts[0]), x, xa, xb, c, ca, cb, got, got_a, got_b, cg, gated, got_thin)

    middle = side // 2

    def plus(a, b):
        return (a.astype(F32) + b.astype(F32)).astype(BF)

    def first_half(parts, over_first):
        return over_first(parts[2], 1), over_first(parts[3], -1)

    def second_half(parts, got):
        o1 = jnp.concatenate([plus(parts[1][:middle], got[0]), parts[1][middle:]], axis=0)
        o3 = jnp.concatenate([parts[4][:middle], plus(parts[4][middle:], got[1])], axis=0)
        return o1, o3

    def mine(parts, got, at):
        def one(distance):
            i = (at + distance) % side
            picked = (lax.dynamic_index_in_dim(v, i, 0, False) for v in (parts[0], *got))
            return sum(v.astype(F32) for v in picked)

        return one(0), [one(d).astype(BF) for d in (1, 2, 3)]

    def across(values, over_second):
        return [over_second(v, d + 1) for d, v in enumerate(values)]

    far_next = second_half(far_parts, first_half(far_parts, over_x))

    def far_rows(which):
        return pl.BlockSpec((tile // part, part, hidden), lambda j: (j, which, 0))

    out, back = call(
        partial(rows_kernel, cap),
        (steps,),
        [whole((total, hidden))] * 2 + [up_rows, cols(hidden), far_rows(0), far_rows(1)],
        [cols(6 * cap)] * 2,
        [jax.ShapeDtypeStruct((6 * cap, width), BF)] * 2,
        [],
    )(after(cg, near_parts[0], out_got_m, out_got_p, back_got_m, back_got_p, far_next), gated, up, down, gathered, gathered)

    block = jax.ShapeDtypeStruct((rows, width), BF)
    returns = call(
        partial(return_kernel, groups, cap),
        (steps,),
        [scalars()] + [table_spec] * 2 + [cols(6 * cap), cols(cap), cols(cap)],
        [cols(rows)] * 2,
        [block] * 2,
        [],
    )
    finals = call(
        partial(final_kernel, groups, cap),
        (steps,),
        [scalars(), table_spec, cols(6 * cap), cols(rows), cols(rows)],
        cols(rows),
        block,
        [],
    )
    near_next = second_half(near_parts, after(first_half(near_parts, over_y), out))
    out_m, out_p = returns(
        after(place, far_next, near_next),
        tm, tp, out, out_got_m, out_got_p,
    )
    back_m, back_p = returns(place, tm, tp, back, back_got_m, back_got_p)
    far_got = after((over_x(far_next[0], 1), over_x(far_next[1], -1)), back_m)
    near_got = after((over_y(near_next[0], 1), over_y(near_next[1], -1)), back_m)
    far_own, far_send = mine(far_parts, far_got, row)
    near_own, near_send = mine(near_parts, near_got, col)
    far_sent, near_sent = across(far_send, over_y), across(near_send, over_x)
    layer_out = finals(
        after(place, far_sent, near_send), t0, out, over_z(out_m, -1), over_z(out_p, 1)
    )
    sum_far = far_own + sum(v.astype(F32) for v in far_sent)
    sum_near = near_own + sum(v.astype(F32) for v in near_sent)
    weight = sum_near + over_z(sum_far.astype(BF), half).astype(F32)
    keep = jnp.where(first_core, weight[:part], weight[part:])
    give = jnp.where(first_core, weight[part:], weight[:part])
    other = over_core(give)
    up_grad = jnp.where(first_core, keep, other)
    down_grad = jnp.where(first_core, other, keep)
    token_grad = finals(after(place, give), t0, back, over_z(back_m, -1), over_z(back_p, 1))
    inner = after(inner, layer_out, near_sent)

    from_p, from_m = over_z(inner, -1), over_z(inner, 1)
    from_b, from_a = over_z(inner, -2), over_z(inner, 2)
    table = jnp.stack(
        [inner[0], from_p[1], from_b[3], from_m[7], inner[5], from_p[6], from_a[4], from_m[2]]
    )
    offset = lax.broadcasted_iota(jnp.int32, (groups, 1), 0)

    def gate_of(k):
        hit = ((routes[:, k] - z) % groups)[None, :] == offset
        return jnp.sum(jnp.where(hit, table, 0.0), axis=0)

    gate_grad = jnp.stack([gate_of(0), gate_of(1)], axis=1)
    return (layer_out, token_grad, gate_grad, up_grad[None], down_grad.T[None])


def solution(mesh):
    rows = P(("dp", "expert"), None)
    weights = P("expert", None, None)
    return jax.shard_map(
        local,
        mesh=mesh,
        in_specs=(rows, rows, rows, rows, weights, weights, P("expert", None)),
        out_specs=(rows, rows, rows, P("expert", "dp", None), P("expert", None, "dp")),
        check_vma=False,
    )
```

```python
from functools import partial

import jax
import jax.numpy as jnp
from jax import lax
from jax.experimental import pallas as pl
from jax.experimental.pallas import tpu as pltpu
from jax.sharding import PartitionSpec as P

STEPS = 4
SHARPNESS = 4.0
BF = jnp.bfloat16
F32 = jnp.float32
VMEM_LIMIT = 56 * 1024 * 1024


def dot(a, b, ca, cb):
    return lax.dot_general(a, b, (((ca,), (cb,)), ((), ())), preferred_element_type=F32)


def call(body, grid, in_specs, out_specs, out_shape, scratch):
    return pl.pallas_call(
        body,
        grid=grid,
        in_specs=in_specs,
        out_specs=out_specs,
        out_shape=out_shape,
        scratch_shapes=scratch,
        compiler_params=pltpu.CompilerParams(
            dimension_semantics=("arbitrary",) * len(grid), vmem_limit_bytes=VMEM_LIMIT
        ),
        cost_estimate=pl.CostEstimate(flops=0, bytes_accessed=1 << 16, transcendentals=0),
    )


def whole(shape):
    return pl.BlockSpec(shape, lambda j: (0,) * len(shape))


def scalars():
    return pl.BlockSpec(memory_space=pltpu.SMEM)


def rank_row(table, e, groups):
    return table[pl.ds(lax.rem(e, groups), 1), :]


def gate_row(table, e, groups):
    return table[pl.ds(lax.rem(e, groups) + groups, 1), :]


def hits(table, e, groups, cap):
    slot = lax.broadcasted_iota(jnp.int32, (cap, table.shape[1]), 0).astype(F32)
    return rank_row(table, e, groups) == slot


def one_hot(table, e, groups, cap):
    return jnp.where(hits(table, e, groups, cap), 1.0, 0.0).astype(BF)


def pick_kernel(groups, cap, place, t0, tm, tp, x0, xm, xp, kept, on_m, on_p):
    z = place[0]
    half = groups // 2

    def take(table, off, src):
        return dot(one_hot(table, z + off, groups, cap), src[...], 1, 0).astype(BF)

    on_m[...] = take(tm, 1, xm)
    on_p[...] = take(tp, groups - 1, xp)
    for i, (table, src) in enumerate(((t0, x0), (tm, xm), (tp, xp))):
        kept[i * cap : (i + 1) * cap, :] = take(table, 0, src)
        kept[(3 + i) * cap : (4 + i) * cap, :] = take(table, half, src)


def pick_on_kernel(groups, cap, place, t0, tm, tp, x0, xm, xp, x_m, x_p, kept, on_m, on_p):
    high = pl.ds(cap, cap)
    on_m[:cap, :] = x_m[...]
    on_p[:cap, :] = x_p[...]
    pick_kernel(
        groups, cap, place, t0, tm, tp, x0, xm, xp, kept, on_m.at[high], on_p.at[high]
    )


def neuron(current, leak):
    v = current
    dv = jnp.ones_like(current)
    total = jnp.zeros_like(current)
    grad = jnp.zeros_like(current)
    for step in range(STEPS):
        if step:
            v = leak * v + current
            dv = leak * dv + 1.0
        t = jnp.tanh((0.5 * SHARPNESS) * (v - 1.0))
        spike = 0.5 * t + 0.5
        dspike = (0.25 * SHARPNESS) * (1.0 - t * t) * dv
        v = v - spike
        dv = dv - dspike
        total = total + spike
        grad = grad + dspike
    return total * (1.0 / STEPS), grad * (1.0 / STEPS)


def forward_kernel(x, up, decay, rates, slope):
    weights = up[...].reshape(x.shape[1], decay.shape[1])
    rates[...], slope[...] = neuron(dot(x[...], weights, 1, 0), decay[...])


def gate_rows(pairs, z, groups, cap, gates):
    for i, (table, off) in enumerate(pairs):
        row = jnp.where(hits(table, z + off, groups, cap), gate_row(table, z + off, groups), 0.0)
        gates[i * cap : (i + 1) * cap, :] = jnp.broadcast_to(
            jnp.sum(row, axis=1, keepdims=True), (cap, 128)
        )


def spread_rows(pairs, z, groups, cap, products, inner):
    for i, (table, off) in enumerate(pairs):
        value = jnp.sum(products[i * cap : (i + 1) * cap, :], axis=1, keepdims=True)
        inner[i : i + 1, :] = jnp.sum(
            jnp.where(hits(table, z + off, groups, cap), value, 0.0), axis=0, keepdims=True
        )


def pull_back(rows, core, r, slope, grad, gates, products, cg, gated, send):
    gate = gates[rows, 0:1]
    both = r * grad
    acc = both[:, :128]
    for k in range(1, both.shape[1] // 128):
        acc = acc + both[:, k * 128 : (k + 1) * 128]
    products[rows, :] += acc
    current = (gate * grad * slope).astype(BF)
    scaled = (gate * r).astype(BF)
    cg[rows, :] = current
    gated[rows, :] = scaled
    send[...] = jnp.where(core == 0, scaled, current)


def backward_kernel(
    groups, cap, place, t0, tm, tp, c, down, down_far, rates_n, slope_n, rates_f, slope_f,
    cg, gated, send_n, send_f, inner, gates, products,
):
    z, core = place[0], place[1]
    half = groups // 2
    step = pl.program_id(0)
    three = 3 * cap
    pairs = ((t0, 0), (tm, 0), (tp, 0), (t0, half), (tm, half), (tp, half))

    @pl.when(step == 0)
    def _():
        products[...] = jnp.zeros_like(products)
        gate_rows(pairs, z, groups, cap, gates)

    far = down_far[...].reshape(c.shape[1], down_far.shape[2])
    for low, send, rates, slope, grad in (
        (0, send_n, rates_n, slope_n, dot(c[:three, :], down[...], 1, 1)),
        (three, send_f, rates_f, slope_f, dot(c[three:, :], far, 1, 0)),
    ):
        rows = slice(low, low + three)
        pull_back(
            rows, core, rates[...], slope[...], grad, gates, products, cg, gated, send
        )

    @pl.when(step == pl.num_programs(0) - 1)
    def _():
        spread_rows(pairs, z, groups, cap, products, inner)


def onward_kernel(
    groups, cap, place, ta, tb, a, b, up, down, decay, cg, gated, send, inner,
    x, c, gates, products,
):
    z, core = place[0], place[1]
    step = pl.program_id(0)
    pairs = ((ta, 0), (tb, 0))

    @pl.when(step == 0)
    def _():
        products[...] = jnp.zeros_like(products)
        gate_rows(pairs, z, groups, cap, gates)
        x[:cap, :], x[cap:, :] = a[:cap, :], b[:cap, :]
        c[:cap, :], c[cap:, :] = a[cap:, :], b[cap:, :]

    rates, slope = neuron(dot(x[...], up[...], 1, 0), decay[...])
    grad = dot(c[...], down[...], 1, 1)
    rows = slice(0, 2 * cap)
    pull_back(rows, core, rates, slope, grad, gates, products, cg, gated, send)

    @pl.when(step == pl.num_programs(0) - 1)
    def _():
        spread_rows(pairs, z, groups, cap, products, inner)


def lay_out(x_first, grid_width, where, grads, o0, o1, o2a, o2b, o3):
    step = pl.program_id(0)
    each = o0.shape[1]
    for k in range(2):
        chip = 2 * step + k
        y, x = chip // grid_width, lax.rem(chip, grid_width)
        main, other = (x, y) if x_first else (y, x)
        away = lax.rem(main - where + grid_width, grid_width)
        value = grads[k * each : (k + 1) * each]
        middle = grid_width // 2
        for distance, target in ((0, o0), (1, o1), (3, o3)):

            @pl.when(away == distance)
            def _(target=target, value=value, other=other):
                target[other] = value

        @pl.when((away == 2) & (other < middle))
        def _(value=value, other=other):
            o2a[other] = value

        @pl.when((away == 2) & (other >= middle))
        def _(value=value, other=other):
            o2b[other - middle] = value


def weight_near_kernel(
    cap, side, place, x, c, a, b, got, got_d, cg, gated, cg_d, gated_d, got_thin, got_thin_d,
    o0, o1, o2a, o2b, o3, wide, thin,
):
    first = place[1] == 0
    three, four, five = 3 * cap, 4 * cap, 5 * cap
    eight = five + three

    @pl.when(pl.program_id(0) == 0)
    def _():
        thin[:three, :] = jnp.where(first, cg[...], gated[...])
        thin[three:five, :] = jnp.where(first, cg_d[...], gated_d[...])
        thin[five:eight, :] = got_thin[...]
        thin[eight:, :] = got_thin_d[...]

    wide[:three, :] = jnp.where(first, x[...], c[...])
    wide[three:four, :] = jnp.where(first, a[:cap, :], a[cap:, :])
    wide[four:five, :] = jnp.where(first, b[:cap, :], b[cap:, :])
    wide[five:eight, :] = got[...]
    wide[eight:, :] = got_d[...]
    grads = dot(wide[...], thin[...], 0, 0).astype(BF)
    lay_out(False, side, place[2], grads, o0, o1, o2a, o2b, o3)


def weight_far_kernel(
    cap, side, place, x, c, got, cg, gated, got_thin, o0, o1, o2a, o2b, o3, wide, thin
):
    first = place[1] == 0
    three = 3 * cap

    @pl.when(pl.program_id(0) == 0)
    def _():
        thin[:three, :] = jnp.where(first, cg[...], gated[...])
        thin[three:, :] = got_thin[...]

    wide[:three, :] = jnp.where(first, x[...], c[...])
    wide[three:, :] = got[...]
    grads = dot(wide[...], thin[...], 0, 0).astype(BF)
    lay_out(True, side, place[3], grads, o0, o1, o2a, o2b, o3)


def rows_kernel(
    cap, cg, gated, cg_d, gated_d, up, down, up_far, down_far, out, back, on_a, on_b
):
    hidden = up.shape[1]
    three, four = 3 * cap, 4 * cap
    uf = up_far[...].reshape(up.shape[0], hidden)
    df = down_far[...].reshape(up.shape[0], hidden)
    near = jnp.concatenate([gated[:three, :], gated_d[...]], axis=0)
    values = dot(near, down[...], 1, 0).astype(BF)
    out[:three, :], on_a[:cap, :], on_b[:cap, :] = values[:three], values[three:four], values[four:]
    out[three:, :] = dot(gated[three:, :], df, 1, 1).astype(BF)
    near = jnp.concatenate([cg[:three, :], cg_d[...]], axis=0)
    values = dot(near, up[...], 1, 1).astype(BF)
    back[:three, :], on_a[cap:, :], on_b[cap:, :] = values[:three], values[three:four], values[four:]
    back[three:, :] = dot(cg[three:, :], uf, 1, 1).astype(BF)


def return_kernel(groups, cap, place, tm, tp, rows, got_m, got_p, to_m, to_p):
    z = place[0]
    half = groups // 2

    def put(table, off, values):
        return dot(one_hot(table, z + off, groups, cap), values, 0, 0)

    for table, i, extra, got, to in (
        (tm, 1, 1, got_m, to_m),
        (tp, 2, groups - 1, got_p, to_p),
    ):
        total = put(table, 0, rows[i * cap : (i + 1) * cap, :])
        total += put(table, half, rows[(3 + i) * cap : (4 + i) * cap, :])
        total += put(table, extra, got[...])
        to[...] = total.astype(BF)


def final_kernel(groups, cap, place, t0, rows, a, b, result):
    z = place[0]
    half = groups // 2
    total = dot(one_hot(t0, z, groups, cap), rows[:cap, :], 0, 0)
    total += dot(one_hot(t0, z + half, groups, cap), rows[3 * cap : 4 * cap, :], 0, 0)
    total += a[...].astype(F32) + b[...].astype(F32)
    result[...] = total.astype(BF)


def local(tokens, cotangent, routes, gate_probs, w_up, w_down, decay_rate):
    rows, width = tokens.shape
    hidden = w_up.shape[2]
    groups = lax.axis_size("expert")
    data = lax.axis_size("dp")
    half = groups // 2
    cap = 3 * rows // groups
    z = lax.axis_index("expert")
    dp = lax.axis_index("dp")
    core = dp % 2
    first_core = core == 0
    chips = data // 2
    side = 4
    row, col = dp // (2 * side), (dp // 2) % side
    place = jnp.stack([z, core, row, col]).astype(jnp.int32)
    up, down = w_up[0], w_down[0]

    def over_z(x, step):
        return lax.ppermute(x, "expert", [(i, (i + step) % groups) for i in range(groups)])

    def over_core(x):
        return lax.ppermute(x, "dp", [(i, i ^ 1) for i in range(data)])

    def over_x(x, step):
        return lax.ppermute(
            x,
            "dp",
            [(i, i - 2 * (i // 2 % side) + 2 * ((i // 2 + step) % side)) for i in range(data)],
        )

    def over_y(x, step):
        return lax.ppermute(
            x, "dp", [(i, (i + 2 * side * step) % data) for i in range(data)]
        )

    def after(x, *done):
        return lax.optimization_barrier((x, *done))[0]

    part = width // data
    up_slice = lax.dynamic_slice_in_dim(up, dp * part, part, 0)
    down_slice = lax.dynamic_slice_in_dim(down, dp * part, part, 1).T
    slices = over_z(jnp.concatenate([up_slice, down_slice], axis=0), half)
    gathered = lax.all_gather(slices, "dp", axis=0, tiled=False)
    decay_far = over_z(decay_rate, half)

    ids = lax.broadcasted_iota(jnp.int32, (groups, 1), 0)
    first = routes[:, 0][None, :] == ids
    second = routes[:, 1][None, :] == ids
    named = first | second
    tri = (
        lax.broadcasted_iota(jnp.int32, (rows, rows), 0)
        < lax.broadcasted_iota(jnp.int32, (rows, rows), 1)
    ).astype(BF)
    rank = jnp.where(named, dot(named.astype(BF), tri, 1, 0), -1.0)
    gates = jnp.where(first, gate_probs[:, 0][None, :], 0.0) + jnp.where(
        second, gate_probs[:, 1][None, :], 0.0
    )
    t0 = jnp.concatenate([rank, gates], axis=0)
    tm, tp, ta, tb = over_z(t0, 1), over_z(t0, -1), over_z(t0, 2), over_z(t0, -2)

    tokens = after(tokens, slices)
    tok_m, tok_p = over_z(tokens, 1), over_z(tokens, -1)
    cotangent = after(cotangent, tok_m, tok_p, tm, tp, ta, tb, decay_far)
    cot_m, cot_p = over_z(cotangent, 1), over_z(cotangent, -1)

    table_spec = whole((2 * groups, rows))
    tile = 512
    steps = width // tile

    def cols(n):
        return pl.BlockSpec((n, tile), lambda j: (0, j))

    def picks(kernel, on, extra):
        return call(
            partial(kernel, groups, cap),
            (steps,),
            [scalars()] + [table_spec] * 3 + [cols(rows)] * 3 + extra,
            [cols(6 * cap), cols(on), cols(on)],
            [jax.ShapeDtypeStruct((n, width), BF) for n in (6 * cap, on, on)],
            [],
        )

    x, x_m, x_p = picks(pick_kernel, cap, [])(place, t0, tm, tp, tokens, tok_m, tok_p)

    ff = 256
    ff_steps = hidden // ff

    def ff_cols(n):
        return pl.BlockSpec((n, ff), lambda j: (0, j))

    def far_ff(which):
        return pl.BlockSpec((data, part, ff), lambda j: (0, which, j))

    total = 8 * cap

    def half_rows(i):
        return pl.BlockSpec((3 * cap, width), lambda j: (i, 0))

    def forward(half_index, spec, *args):
        return call(
            forward_kernel,
            (ff_steps,),
            [half_rows(half_index), spec, ff_cols(1)],
            [ff_cols(three)] * 2,
            [jax.ShapeDtypeStruct((three, hidden), F32)] * 2,
            [],
        )(*args)

    three = 3 * cap
    rates_n, slope_n = forward(0, ff_cols(width), x, up, decay_rate)
    rates_f, slope_f = forward(1, far_ff(0), after(x, rates_n), gathered, decay_far)
    c, on_m, on_p = picks(pick_on_kernel, 2 * cap, [cols(cap)] * 2)(
        after(place, rates_f), t0, tm, tp, cotangent, cot_m, cot_p, x_m, x_p
    )
    on_a, on_b = over_z(on_m, 1), over_z(on_p, -1)
    got = over_core(jnp.where(first_core, c, x))

    down_ff = pl.BlockSpec((ff, width), lambda j: (j, 0))
    cg, gated, send_n, send_f, inner = call(
        partial(backward_kernel, groups, cap),
        (ff_steps,),
        [scalars()] + [table_spec] * 3 + [whole((6 * cap, width)), down_ff, far_ff(1)]
        + [ff_cols(three)] * 4,
        [ff_cols(n * cap) for n in (6, 6, 3, 3)] + [whole((6, rows))],
        [jax.ShapeDtypeStruct((n * cap, hidden), BF) for n in (6, 6, 3, 3)]
        + [jax.ShapeDtypeStruct((6, rows), F32)],
        [pltpu.VMEM((6 * cap, 128), F32)] * 2,
    )(place, t0, tm, tp, c, down, gathered, rates_n, slope_n, rates_f, slope_f)
    got_thin_f = over_core(send_f)
    got_thin = over_core(after(send_n, got_thin_f))

    span = 2 * width // chips

    def span_cols(n, i=0):
        return pl.BlockSpec((n, span), lambda j: (i, j))

    def thin_rows(n, i=0):
        return pl.BlockSpec((n, hidden), lambda j: (i, 0))

    each = width // chips
    counts = (side, side, side // 2, side // 2, side)
    laid = [whole((n, each, hidden)) for n in counts]
    laid_shapes = [jax.ShapeDtypeStruct((n, each, hidden), BF) for n in counts]
    far_parts = call(
        partial(weight_far_kernel, cap, side),
        (chips // 2,),
        [scalars()] + [span_cols(three, 1)] * 3 + [thin_rows(three, 1)] * 2 + [thin_rows(three)],
        laid,
        laid_shapes,
        [pltpu.VMEM((6 * cap, span), BF), pltpu.VMEM((6 * cap, hidden), BF)],
    )(place, x, c, got, cg, gated, got_thin_f)
    cg_d, gated_d, send_d, inner_d = call(
        partial(onward_kernel, groups, cap),
        (ff_steps,),
        [scalars()] + [table_spec] * 2 + [whole((2 * cap, width))] * 2
        + [ff_cols(width), down_ff, ff_cols(1)],
        [ff_cols(2 * cap)] * 3 + [whole((2, rows))],
        [jax.ShapeDtypeStruct((2 * cap, hidden), BF)] * 3
        + [jax.ShapeDtypeStruct((2, rows), F32)],
        [pltpu.VMEM((2 * cap, width), BF)] * 2 + [pltpu.VMEM((2 * cap, 128), F32)] * 2,
    )(after(place, far_parts[0]), ta, tb, on_a, on_b, up, down, decay_rate)
    got_thin_d = over_core(send_d)
    far_a, far_b = after((on_a, on_b), cg_d)
    got_d = over_core(
        jnp.concatenate([jnp.where(first_core, v[cap:], v[:cap]) for v in (far_a, far_b)], axis=0)
    )

    middle = side // 2

    def plus(a, b):
        return (a.astype(F32) + b.astype(F32)).astype(BF)

    def first_half(parts, over_first):
        return over_first(parts[2], 1), over_first(parts[3], -1)

    def second_half(parts, got):
        low = ((0, middle), (0, 0), (0, 0))
        high = ((middle, 0), (0, 0), (0, 0))
        o1, o3 = plus(parts[1], jnp.pad(got[0], low)), plus(parts[4], jnp.pad(got[1], high))
        return o1, o3

    def mine(parts, got, at):
        def one(distance):
            i = (at + distance) % side
            picked = (lax.dynamic_index_in_dim(v, i, 0, False) for v in (parts[0], *got))
            return sum(v.astype(F32) for v in picked)

        return one(0), [one(d).astype(BF) for d in (1, 2, 3)]

    def across(values, over_second):
        return [over_second(v, d + 1) for d, v in enumerate(values)]

    far_next = second_half(far_parts, first_half(far_parts, over_x))

    def far_rows(which):
        return pl.BlockSpec((tile // part, part, hidden), lambda j: (j, which, 0))

    up_rows = pl.BlockSpec((tile, hidden), lambda j: (j, 0))
    row_shapes = [jax.ShapeDtypeStruct((n * cap, width), BF) for n in (6, 6, 2, 2)]
    out, back, to_a, to_b = call(
        partial(rows_kernel, cap),
        (steps,),
        [whole((6 * cap, hidden))] * 2 + [whole((2 * cap, hidden))] * 2
        + [up_rows, cols(hidden), far_rows(0), far_rows(1)],
        [cols(6 * cap), cols(6 * cap), cols(2 * cap), cols(2 * cap)],
        row_shapes,
        [],
    )(after(cg, far_next), gated, cg_d, gated_d, up, down, gathered, gathered)
    got_m, got_p = over_z(to_a, -1), over_z(to_b, 1)
    near_parts = call(
        partial(weight_near_kernel, cap, side),
        (chips // 2,),
        [scalars()] + [span_cols(three)] * 2 + [span_cols(2 * cap)] * 2
        + [span_cols(three), span_cols(2 * cap)]
        + [thin_rows(three)] * 2 + [thin_rows(2 * cap)] * 2 + [thin_rows(three), thin_rows(2 * cap)],
        laid,
        laid_shapes,
        [pltpu.VMEM((10 * cap, span), BF), pltpu.VMEM((10 * cap, hidden), BF)],
    )(
        after(place, out), x, c, on_a, on_b, got, got_d,
        cg, gated, cg_d, gated_d, got_thin, got_thin_d,
    )

    block = jax.ShapeDtypeStruct((rows, width), BF)
    def onward(which):
        return pl.BlockSpec((cap, tile), lambda j: (which, j))

    returns = lambda which: call(
        partial(return_kernel, groups, cap),
        (steps,),
        [scalars()] + [table_spec] * 2 + [cols(6 * cap), onward(which), onward(which)],
        [cols(rows)] * 2,
        [block] * 2,
        [],
    )
    finals = call(
        partial(final_kernel, groups, cap),
        (steps,),
        [scalars(), table_spec, cols(6 * cap), cols(rows), cols(rows)],
        cols(rows),
        block,
        [],
    )
    out_m, out_p = returns(0)(place, tm, tp, after(out, near_parts[0]), got_m, got_p)
    back_m, back_p = returns(1)(after(place, out_m), tm, tp, back, got_m, got_p)
    near_next = second_half(near_parts, after(first_half(near_parts, over_y), back_m))
    far_got = after((over_x(far_next[0], 1), over_x(far_next[1], -1)), back_m)
    near_got = (over_y(near_next[0], 1), over_y(near_next[1], -1))
    far_own, far_send = mine(far_parts, far_got, row)
    homes = (over_z(out_m, -1), over_z(out_p, 1))
    near_own, near_send = mine(near_parts, after(near_got, *homes), col)
    far_sent, near_sent = across(far_send, over_y), across(near_send, over_x)
    layer_out = finals(after(place, near_send), t0, out, *homes)
    sum_far = far_own + sum(v.astype(F32) for v in far_sent)
    back_m, back_p = after((back_m, back_p), sum_far)
    sum_near = near_own + sum(v.astype(F32) for v in near_sent)
    weight = sum_near + over_z(sum_far.astype(BF), half).astype(F32)
    keep = jnp.where(first_core, weight[:part], weight[part:])
    give = jnp.where(first_core, weight[part:], weight[:part])
    other = over_core(give)
    up_grad = jnp.where(first_core, keep, other)
    down_grad = jnp.where(first_core, other, keep)
    token_grad = finals(after(place, give), t0, back, over_z(back_m, -1), over_z(back_p, 1))
    inner = jnp.concatenate([inner, inner_d], axis=0)
    inners = lax.all_gather(inner, "expert", axis=0, tiled=False)

    def of(step, i):
        return lax.dynamic_slice(inners, ((z + step) % groups, i, 0), (1, 1, rows))[0, 0]

    table = jnp.stack(
        [of(0, 0), of(1, 1), of(2, 6), of(-1, 5), of(0, 3), of(1, 4), of(-2, 7), of(-1, 2)]
    )
    offset = lax.broadcasted_iota(jnp.int32, (groups, 1), 0)

    def gate_of(k):
        hit = ((routes[:, k] - z) % groups)[None, :] == offset
        return jnp.sum(jnp.where(hit, table, 0.0), axis=0)

    gate_grad = jnp.stack([gate_of(0), gate_of(1)], axis=1)
    return (layer_out, token_grad, gate_grad, up_grad[None], down_grad.T[None])


def solution(mesh):
    rows = P(("dp", "expert"), None)
    weights = P("expert", None, None)
    return jax.shard_map(
        local,
        mesh=mesh,
        in_specs=(rows, rows, rows, rows, weights, weights, P("expert", None)),
        out_specs=(rows, rows, rows, P("expert", "dp", None), P("expert", None, "dp")),
        check_vma=False,
    )
```

```python
from functools import partial

import jax
import jax.numpy as jnp
from jax import lax
from jax.experimental import pallas as pl
from jax.experimental.pallas import tpu as pltpu
from jax.sharding import PartitionSpec as P

STEPS = 4
SHARPNESS = 4.0
BF = jnp.bfloat16
F32 = jnp.float32
VMEM_LIMIT = 56 * 1024 * 1024


def dot(a, b, ca, cb):
    return lax.dot_general(a, b, (((ca,), (cb,)), ((), ())), preferred_element_type=F32)


def call(body, grid, in_specs, out_specs, out_shape, scratch):
    return pl.pallas_call(
        body,
        grid=grid,
        in_specs=in_specs,
        out_specs=out_specs,
        out_shape=out_shape,
        scratch_shapes=scratch,
        compiler_params=pltpu.CompilerParams(
            dimension_semantics=("arbitrary",) * len(grid), vmem_limit_bytes=VMEM_LIMIT
        ),
        cost_estimate=pl.CostEstimate(flops=0, bytes_accessed=1 << 16, transcendentals=0),
    )


def whole(shape):
    return pl.BlockSpec(shape, lambda j: (0,) * len(shape))


def scalars():
    return pl.BlockSpec(memory_space=pltpu.SMEM)


def rank_row(table, e, groups):
    return table[pl.ds(lax.rem(e, groups), 1), :]


def gate_row(table, e, groups):
    return table[pl.ds(lax.rem(e, groups) + groups, 1), :]


def hits(table, e, groups, cap):
    slot = lax.broadcasted_iota(jnp.int32, (cap, table.shape[1]), 0).astype(F32)
    return rank_row(table, e, groups) == slot


def one_hot(table, e, groups, cap):
    return jnp.where(hits(table, e, groups, cap), 1.0, 0.0).astype(BF)


def pick_kernel(groups, cap, place, t0, tm, tp, x0, xm, xp, kept, on_m, on_p):
    z = place[0]
    half = groups // 2

    def take(table, off, src):
        return dot(one_hot(table, z + off, groups, cap), src[...], 1, 0).astype(BF)

    on_m[...] = take(tm, 1, xm)
    on_p[...] = take(tp, groups - 1, xp)
    for i, (table, src) in enumerate(((t0, x0), (tm, xm), (tp, xp))):
        kept[i * cap : (i + 1) * cap, :] = take(table, 0, src)
        kept[(3 + i) * cap : (4 + i) * cap, :] = take(table, half, src)


def pick_on_kernel(groups, cap, place, t0, tm, tp, x0, xm, xp, x_m, x_p, kept, on_m, on_p):
    high = pl.ds(cap, cap)
    on_m[:cap, :] = x_m[...]
    on_p[:cap, :] = x_p[...]
    pick_kernel(
        groups, cap, place, t0, tm, tp, x0, xm, xp, kept, on_m.at[high], on_p.at[high]
    )


def neuron(current, leak):
    v = current
    dv = jnp.ones_like(current)
    total = jnp.zeros_like(current)
    grad = jnp.zeros_like(current)
    for step in range(STEPS):
        if step:
            v = leak * v + current
            dv = leak * dv + 1.0
        t = jnp.tanh((0.5 * SHARPNESS) * (v - 1.0))
        spike = 0.5 * t + 0.5
        dspike = (0.25 * SHARPNESS) * (1.0 - t * t) * dv
        v = v - spike
        dv = dv - dspike
        total = total + spike
        grad = grad + dspike
    return total * (1.0 / STEPS), grad * (1.0 / STEPS)


def forward_kernel(x, up, decay, rates, slope):
    weights = up[...].reshape(x.shape[1], decay.shape[1])
    rates[...], slope[...] = neuron(dot(x[...], weights, 1, 0), decay[...])


def gate_rows(pairs, z, groups, cap, gates):
    for i, (table, off) in enumerate(pairs):
        row = jnp.where(hits(table, z + off, groups, cap), gate_row(table, z + off, groups), 0.0)
        gates[i * cap : (i + 1) * cap, :] = jnp.broadcast_to(
            jnp.sum(row, axis=1, keepdims=True), (cap, 128)
        )


def spread_rows(pairs, z, groups, cap, products, inner):
    for i, (table, off) in enumerate(pairs):
        value = jnp.sum(products[i * cap : (i + 1) * cap, :], axis=1, keepdims=True)
        inner[i : i + 1, :] = jnp.sum(
            jnp.where(hits(table, z + off, groups, cap), value, 0.0), axis=0, keepdims=True
        )


def pull_back(rows, core, r, slope, grad, gates, products, cg, gated, send):
    gate = gates[rows, 0:1]
    both = r * grad
    acc = both[:, :128]
    for k in range(1, both.shape[1] // 128):
        acc = acc + both[:, k * 128 : (k + 1) * 128]
    products[rows, :] += acc
    current = (gate * grad * slope).astype(BF)
    scaled = (gate * r).astype(BF)
    cg[rows, :] = current
    gated[rows, :] = scaled
    send[...] = jnp.where(core == 0, scaled, current)


def backward_kernel(
    groups, cap, place, t0, tm, tp, c, down, down_far, rates_n, slope_n, rates_f, slope_f,
    cg, gated, send_n, send_f, inner, gates, products,
):
    z, core = place[0], place[1]
    half = groups // 2
    step = pl.program_id(0)
    three = 3 * cap
    pairs = ((t0, 0), (tm, 0), (tp, 0), (t0, half), (tm, half), (tp, half))

    @pl.when(step == 0)
    def _():
        products[...] = jnp.zeros_like(products)
        gate_rows(pairs, z, groups, cap, gates)

    far = down_far[...].reshape(c.shape[1], down_far.shape[2])
    for low, send, rates, slope, grad in (
        (0, send_n, rates_n, slope_n, dot(c[:three, :], down[...], 1, 1)),
        (three, send_f, rates_f, slope_f, dot(c[three:, :], far, 1, 0)),
    ):
        rows = slice(low, low + three)
        pull_back(
            rows, core, rates[...], slope[...], grad, gates, products, cg, gated, send
        )

    @pl.when(step == pl.num_programs(0) - 1)
    def _():
        spread_rows(pairs, z, groups, cap, products, inner)


def onward_kernel(
    groups, cap, place, ta, tb, a, b, up, down, decay, cg, gated, send, inner,
    x, c, gates, products,
):
    z, core = place[0], place[1]
    step = pl.program_id(0)
    pairs = ((ta, 0), (tb, 0))

    @pl.when(step == 0)
    def _():
        products[...] = jnp.zeros_like(products)
        gate_rows(pairs, z, groups, cap, gates)
        x[:cap, :], x[cap:, :] = a[:cap, :], b[:cap, :]
        c[:cap, :], c[cap:, :] = a[cap:, :], b[cap:, :]

    rates, slope = neuron(dot(x[...], up[...], 1, 0), decay[...])
    grad = dot(c[...], down[...], 1, 1)
    rows = slice(0, 2 * cap)
    pull_back(rows, core, rates, slope, grad, gates, products, cg, gated, send)

    @pl.when(step == pl.num_programs(0) - 1)
    def _():
        spread_rows(pairs, z, groups, cap, products, inner)


def lay_out(x_first, grid_width, where, grads, o0, o1, o2a, o2b, o3):
    step = pl.program_id(0)
    each = o0.shape[1]
    for k in range(2):
        chip = 2 * step + k
        y, x = chip // grid_width, lax.rem(chip, grid_width)
        main, other = (x, y) if x_first else (y, x)
        away = lax.rem(main - where + grid_width, grid_width)
        value = grads[k * each : (k + 1) * each]
        middle = grid_width // 2
        for distance, target in ((0, o0), (1, o1), (3, o3)):

            @pl.when(away == distance)
            def _(target=target, value=value, other=other):
                target[other] = value

        @pl.when((away == 2) & (other < middle))
        def _(value=value, other=other):
            o2a[other] = value

        @pl.when((away == 2) & (other >= middle))
        def _(value=value, other=other):
            o2b[other - middle] = value


def weight_near_kernel(
    cap, side, place, x, c, a, b, got, got_d, cg, gated, cg_d, gated_d, got_thin, got_thin_d,
    o0, o1, o2a, o2b, o3, wide, thin,
):
    first = place[1] == 0
    three, four, five = 3 * cap, 4 * cap, 5 * cap
    eight = five + three

    @pl.when(pl.program_id(0) == 0)
    def _():
        thin[:three, :] = jnp.where(first, cg[...], gated[...])
        thin[three:five, :] = jnp.where(first, cg_d[...], gated_d[...])
        thin[five:eight, :] = got_thin[...]
        thin[eight:, :] = got_thin_d[...]

    wide[:three, :] = jnp.where(first, x[...], c[...])
    wide[three:four, :] = jnp.where(first, a[:cap, :], a[cap:, :])
    wide[four:five, :] = jnp.where(first, b[:cap, :], b[cap:, :])
    wide[five:eight, :] = got[...]
    wide[eight:, :] = got_d[...]
    grads = dot(wide[...], thin[...], 0, 0).astype(BF)
    lay_out(False, side, place[2], grads, o0, o1, o2a, o2b, o3)


def weight_far_kernel(
    cap, side, place, x, c, got, cg, gated, got_thin, o0, o1, o2a, o2b, o3, wide, thin
):
    first = place[1] == 0
    three = 3 * cap

    @pl.when(pl.program_id(0) == 0)
    def _():
        thin[:three, :] = jnp.where(first, cg[...], gated[...])
        thin[three:, :] = got_thin[...]

    wide[:three, :] = jnp.where(first, x[...], c[...])
    wide[three:, :] = got[...]
    grads = dot(wide[...], thin[...], 0, 0).astype(BF)
    lay_out(True, side, place[3], grads, o0, o1, o2a, o2b, o3)


def rows_kernel(
    cap, cg, gated, cg_d, gated_d, up, down, up_far, down_far, out, back, on_a, on_b
):
    hidden = up.shape[1]
    three, four = 3 * cap, 4 * cap
    uf = up_far[...].reshape(up.shape[0], hidden)
    df = down_far[...].reshape(up.shape[0], hidden)
    near = jnp.concatenate([gated[:three, :], gated_d[...]], axis=0)
    values = dot(near, down[...], 1, 0).astype(BF)
    out[:three, :], on_a[:cap, :], on_b[:cap, :] = values[:three], values[three:four], values[four:]
    out[three:, :] = dot(gated[three:, :], df, 1, 1).astype(BF)
    near = jnp.concatenate([cg[:three, :], cg_d[...]], axis=0)
    values = dot(near, up[...], 1, 1).astype(BF)
    back[:three, :], on_a[cap:, :], on_b[cap:, :] = values[:three], values[three:four], values[four:]
    back[three:, :] = dot(cg[three:, :], uf, 1, 1).astype(BF)


def return_kernel(groups, cap, place, tm, tp, rows, got_m, got_p, to_m, to_p):
    z = place[0]
    half = groups // 2

    def put(table, off, values):
        return dot(one_hot(table, z + off, groups, cap), values, 0, 0)

    for table, i, extra, got, to in (
        (tm, 1, 1, got_m, to_m),
        (tp, 2, groups - 1, got_p, to_p),
    ):
        total = put(table, 0, rows[i * cap : (i + 1) * cap, :])
        total += put(table, half, rows[(3 + i) * cap : (4 + i) * cap, :])
        total += put(table, extra, got[...])
        to[...] = total.astype(BF)


def final_kernel(groups, cap, place, t0, rows, a, b, result):
    z = place[0]
    half = groups // 2
    total = dot(one_hot(t0, z, groups, cap), rows[:cap, :], 0, 0)
    total += dot(one_hot(t0, z + half, groups, cap), rows[3 * cap : 4 * cap, :], 0, 0)
    total += a[...].astype(F32) + b[...].astype(F32)
    result[...] = total.astype(BF)


def local(tokens, cotangent, routes, gate_probs, w_up, w_down, decay_rate):
    rows, width = tokens.shape
    hidden = w_up.shape[2]
    groups = lax.axis_size("expert")
    data = lax.axis_size("dp")
    half = groups // 2
    cap = 3 * rows // groups
    z = lax.axis_index("expert")
    dp = lax.axis_index("dp")
    core = dp % 2
    first_core = core == 0
    chips = data // 2
    side = 4
    row, col = dp // (2 * side), (dp // 2) % side
    place = jnp.stack([z, core, row, col]).astype(jnp.int32)
    up, down = w_up[0], w_down[0]

    def over_z(x, step):
        return lax.ppermute(x, "expert", [(i, (i + step) % groups) for i in range(groups)])

    def over_core(x):
        return lax.ppermute(x, "dp", [(i, i ^ 1) for i in range(data)])

    def over_x(x, step):
        return lax.ppermute(
            x,
            "dp",
            [(i, i - 2 * (i // 2 % side) + 2 * ((i // 2 + step) % side)) for i in range(data)],
        )

    def over_y(x, step):
        return lax.ppermute(
            x, "dp", [(i, (i + 2 * side * step) % data) for i in range(data)]
        )

    def after(x, *done):
        return lax.optimization_barrier((x, *done))[0]

    part = width // data
    up_slice = lax.dynamic_slice_in_dim(up, dp * part, part, 0)
    down_slice = lax.dynamic_slice_in_dim(down, dp * part, part, 1).T
    slices = over_z(jnp.concatenate([up_slice, down_slice], axis=0), half)
    gathered = lax.all_gather(slices, "dp", axis=0, tiled=False)
    decay_far = over_z(decay_rate, half)

    ids = lax.broadcasted_iota(jnp.int32, (groups, 1), 0)
    first = routes[:, 0][None, :] == ids
    second = routes[:, 1][None, :] == ids
    named = first | second
    tri = (
        lax.broadcasted_iota(jnp.int32, (rows, rows), 0)
        < lax.broadcasted_iota(jnp.int32, (rows, rows), 1)
    ).astype(BF)
    rank = jnp.where(named, dot(named.astype(BF), tri, 1, 0), -1.0)
    gates = jnp.where(first, gate_probs[:, 0][None, :], 0.0) + jnp.where(
        second, gate_probs[:, 1][None, :], 0.0
    )
    t0 = jnp.concatenate([rank, gates], axis=0)
    tm, tp, ta, tb = over_z(t0, 1), over_z(t0, -1), over_z(t0, 2), over_z(t0, -2)

    tokens = after(tokens, slices)
    tok_m, tok_p = over_z(tokens, 1), over_z(tokens, -1)
    cotangent = after(cotangent, tok_m, tok_p, tm, tp, ta, tb, decay_far)
    cot_m, cot_p = over_z(cotangent, 1), over_z(cotangent, -1)

    table_spec = whole((2 * groups, rows))
    tile = 512
    steps = width // tile

    def cols(n):
        return pl.BlockSpec((n, tile), lambda j: (0, j))

    def picks(kernel, on, extra):
        return call(
            partial(kernel, groups, cap),
            (steps,),
            [scalars()] + [table_spec] * 3 + [cols(rows)] * 3 + extra,
            [cols(6 * cap), cols(on), cols(on)],
            [jax.ShapeDtypeStruct((n, width), BF) for n in (6 * cap, on, on)],
            [],
        )

    x, x_m, x_p = picks(pick_kernel, cap, [])(place, t0, tm, tp, tokens, tok_m, tok_p)

    ff = 256
    ff_steps = hidden // ff

    def ff_cols(n):
        return pl.BlockSpec((n, ff), lambda j: (0, j))

    def far_ff(which):
        return pl.BlockSpec((data, part, ff), lambda j: (0, which, j))

    total = 8 * cap

    def half_rows(i):
        return pl.BlockSpec((3 * cap, width), lambda j: (i, 0))

    def forward(half_index, spec, *args):
        return call(
            forward_kernel,
            (ff_steps,),
            [half_rows(half_index), spec, ff_cols(1)],
            [ff_cols(three)] * 2,
            [jax.ShapeDtypeStruct((three, hidden), F32)] * 2,
            [],
        )(*args)

    three = 3 * cap
    rates_n, slope_n = forward(0, ff_cols(width), x, up, decay_rate)
    rates_f, slope_f = forward(1, far_ff(0), after(x, rates_n), gathered, decay_far)
    c, on_m, on_p = picks(pick_on_kernel, 2 * cap, [cols(cap)] * 2)(
        after(place, rates_f), t0, tm, tp, cotangent, cot_m, cot_p, x_m, x_p
    )
    on_a, on_b = over_z(on_m, 1), over_z(on_p, -1)
    got = over_core(jnp.where(first_core, c, x))

    down_ff = pl.BlockSpec((ff, width), lambda j: (j, 0))
    cg, gated, send_n, send_f, inner = call(
        partial(backward_kernel, groups, cap),
        (ff_steps,),
        [scalars()] + [table_spec] * 3 + [whole((6 * cap, width)), down_ff, far_ff(1)]
        + [ff_cols(three)] * 4,
        [ff_cols(n * cap) for n in (6, 6, 3, 3)] + [whole((6, rows))],
        [jax.ShapeDtypeStruct((n * cap, hidden), BF) for n in (6, 6, 3, 3)]
        + [jax.ShapeDtypeStruct((6, rows), F32)],
        [pltpu.VMEM((6 * cap, 128), F32)] * 2,
    )(place, t0, tm, tp, c, down, gathered, rates_n, slope_n, rates_f, slope_f)
    from_p, from_m = over_z(inner, -1), over_z(inner, 1)
    got_thin_f = over_core(send_f)
    got_thin = over_core(after(send_n, got_thin_f))

    span = 2 * width // chips

    def span_cols(n, i=0):
        return pl.BlockSpec((n, span), lambda j: (i, j))

    def thin_rows(n, i=0):
        return pl.BlockSpec((n, hidden), lambda j: (i, 0))

    each = width // chips
    counts = (side, side, side // 2, side // 2, side)
    laid = [whole((n, each, hidden)) for n in counts]
    laid_shapes = [jax.ShapeDtypeStruct((n, each, hidden), BF) for n in counts]
    far_parts = call(
        partial(weight_far_kernel, cap, side),
        (chips // 2,),
        [scalars()] + [span_cols(three, 1)] * 3 + [thin_rows(three, 1)] * 2 + [thin_rows(three)],
        laid,
        laid_shapes,
        [pltpu.VMEM((6 * cap, span), BF), pltpu.VMEM((6 * cap, hidden), BF)],
    )(place, x, c, got, cg, gated, got_thin_f)
    cg_d, gated_d, send_d, inner_d = call(
        partial(onward_kernel, groups, cap),
        (ff_steps,),
        [scalars()] + [table_spec] * 2 + [whole((2 * cap, width))] * 2
        + [ff_cols(width), down_ff, ff_cols(1)],
        [ff_cols(2 * cap)] * 3 + [whole((2, rows))],
        [jax.ShapeDtypeStruct((2 * cap, hidden), BF)] * 3
        + [jax.ShapeDtypeStruct((2, rows), F32)],
        [pltpu.VMEM((2 * cap, width), BF)] * 2 + [pltpu.VMEM((2 * cap, 128), F32)] * 2,
    )(after(place, far_parts[0]), ta, tb, on_a, on_b, up, down, decay_rate)
    from_b, from_a = over_z(inner_d, -2), over_z(inner_d, 2)
    got_thin_d = over_core(send_d)
    far_a, far_b = after((on_a, on_b), cg_d)
    got_d = over_core(
        jnp.concatenate([jnp.where(first_core, v[cap:], v[:cap]) for v in (far_a, far_b)], axis=0)
    )

    middle = side // 2

    def plus(a, b):
        return (a.astype(F32) + b.astype(F32)).astype(BF)

    def first_half(parts, over_first):
        return over_first(parts[2], 1), over_first(parts[3], -1)

    def second_half(parts, got):
        low = ((0, middle), (0, 0), (0, 0))
        high = ((middle, 0), (0, 0), (0, 0))
        o1, o3 = plus(parts[1], jnp.pad(got[0], low)), plus(parts[4], jnp.pad(got[1], high))
        return o1, o3

    def mine(parts, got, at):
        def one(distance):
            i = (at + distance) % side
            picked = (lax.dynamic_index_in_dim(v, i, 0, False) for v in (parts[0], *got))
            return sum(v.astype(F32) for v in picked)

        return one(0), [one(d).astype(BF) for d in (1, 2, 3)]

    def across(values, over_second):
        return [over_second(v, d + 1) for d, v in enumerate(values)]

    far_next = second_half(far_parts, first_half(far_parts, over_x))

    def far_rows(which):
        return pl.BlockSpec((tile // part, part, hidden), lambda j: (j, which, 0))

    up_rows = pl.BlockSpec((tile, hidden), lambda j: (j, 0))
    row_shapes = [jax.ShapeDtypeStruct((n * cap, width), BF) for n in (6, 6, 2, 2)]
    out, back, to_a, to_b = call(
        partial(rows_kernel, cap),
        (steps,),
        [whole((6 * cap, hidden))] * 2 + [whole((2 * cap, hidden))] * 2
        + [up_rows, cols(hidden), far_rows(0), far_rows(1)],
        [cols(6 * cap), cols(6 * cap), cols(2 * cap), cols(2 * cap)],
        row_shapes,
        [],
    )(after(cg, far_next, from_p, from_m, from_b, from_a), gated, cg_d, gated_d, up, down, gathered, gathered)
    got_m, got_p = over_z(to_a, -1), over_z(to_b, 1)
    near_parts = call(
        partial(weight_near_kernel, cap, side),
        (chips // 2,),
        [scalars()] + [span_cols(three)] * 2 + [span_cols(2 * cap)] * 2
        + [span_cols(three), span_cols(2 * cap)]
        + [thin_rows(three)] * 2 + [thin_rows(2 * cap)] * 2 + [thin_rows(three), thin_rows(2 * cap)],
        laid,
        laid_shapes,
        [pltpu.VMEM((10 * cap, span), BF), pltpu.VMEM((10 * cap, hidden), BF)],
    )(
        after(place, out), x, c, on_a, on_b, got, got_d,
        cg, gated, cg_d, gated_d, got_thin, got_thin_d,
    )

    block = jax.ShapeDtypeStruct((rows, width), BF)
    def onward(which):
        return pl.BlockSpec((cap, tile), lambda j: (which, j))

    returns = lambda which: call(
        partial(return_kernel, groups, cap),
        (steps,),
        [scalars()] + [table_spec] * 2 + [cols(6 * cap), onward(which), onward(which)],
        [cols(rows)] * 2,
        [block] * 2,
        [],
    )
    finals = call(
        partial(final_kernel, groups, cap),
        (steps,),
        [scalars(), table_spec, cols(6 * cap), cols(rows), cols(rows)],
        cols(rows),
        block,
        [],
    )
    out_m, out_p = returns(0)(place, tm, tp, after(out, near_parts[0]), got_m, got_p)
    back_m, back_p = returns(1)(after(place, out_m), tm, tp, back, got_m, got_p)
    far_got = after((over_x(far_next[0], 1), over_x(far_next[1], -1)), back_m)
    far_own, far_send = mine(far_parts, far_got, row)
    far_sent = across(far_send, over_y)
    homes = (over_z(out_m, -1), over_z(out_p, 1))
    near_next = second_half(
        near_parts, after(first_half(near_parts, over_y), back_m, far_sent, homes)
    )
    near_got = (over_y(near_next[0], 1), over_y(near_next[1], -1))
    near_own, near_send = mine(near_parts, near_got, col)
    near_sent = across(near_send, over_x)
    layer_out = finals(after(place, near_send), t0, out, *homes)
    sum_far = far_own + sum(v.astype(F32) for v in far_sent)
    back_m, back_p = after((back_m, back_p), sum_far)
    sum_near = near_own + sum(v.astype(F32) for v in near_sent)
    weight = sum_near + over_z(sum_far.astype(BF), half).astype(F32)
    keep = jnp.where(first_core, weight[:part], weight[part:])
    give = jnp.where(first_core, weight[part:], weight[:part])
    other = over_core(give)
    up_grad = jnp.where(first_core, keep, other)
    down_grad = jnp.where(first_core, other, keep)
    token_grad = finals(after(place, give), t0, back, over_z(back_m, -1), over_z(back_p, 1))
    table = jnp.stack(
        [inner[0], from_p[1], from_b[0], from_m[5], inner[3], from_p[4], from_a[1], from_m[2]]
    )
    offset = lax.broadcasted_iota(jnp.int32, (groups, 1), 0)

    def gate_of(k):
        hit = ((routes[:, k] - z) % groups)[None, :] == offset
        return jnp.sum(jnp.where(hit, table, 0.0), axis=0)

    gate_grad = jnp.stack([gate_of(0), gate_of(1)], axis=1)
    return (layer_out, token_grad, gate_grad, up_grad[None], down_grad.T[None])


def solution(mesh):
    rows = P(("dp", "expert"), None)
    weights = P("expert", None, None)
    return jax.shard_map(
        local,
        mesh=mesh,
        in_specs=(rows, rows, rows, rows, weights, weights, P("expert", None)),
        out_specs=(rows, rows, rows, P("expert", "dp", None), P("expert", None, "dp")),
        check_vma=False,
    )
```

```python
from functools import partial

import jax
import jax.numpy as jnp
from jax import lax
from jax.experimental import pallas as pl
from jax.experimental.pallas import tpu as pltpu
from jax.sharding import PartitionSpec as P

STEPS = 4
SHARPNESS = 4.0
BF = jnp.bfloat16
F32 = jnp.float32
VMEM_LIMIT = 56 * 1024 * 1024


def dot(a, b, ca, cb):
    return lax.dot_general(a, b, (((ca,), (cb,)), ((), ())), preferred_element_type=F32)


def call(body, grid, in_specs, out_specs, out_shape, scratch):
    return pl.pallas_call(
        body,
        grid=grid,
        in_specs=in_specs,
        out_specs=out_specs,
        out_shape=out_shape,
        scratch_shapes=scratch,
        compiler_params=pltpu.CompilerParams(
            dimension_semantics=("arbitrary",) * len(grid), vmem_limit_bytes=VMEM_LIMIT
        ),
        cost_estimate=pl.CostEstimate(flops=0, bytes_accessed=1 << 16, transcendentals=0),
    )


def whole(shape):
    return pl.BlockSpec(shape, lambda j: (0,) * len(shape))


def scalars():
    return pl.BlockSpec(memory_space=pltpu.SMEM)


def rank_row(table, e, groups):
    return table[pl.ds(lax.rem(e, groups), 1), :]


def gate_row(table, e, groups):
    return table[pl.ds(lax.rem(e, groups) + groups, 1), :]


def hits(table, e, groups, cap):
    slot = lax.broadcasted_iota(jnp.int32, (cap, table.shape[1]), 0).astype(F32)
    return rank_row(table, e, groups) == slot


def one_hot(table, e, groups, cap):
    return jnp.where(hits(table, e, groups, cap), 1.0, 0.0).astype(BF)


def pick_kernel(groups, cap, place, t0, tm, tp, x0, xm, xp, kept, on_m, on_p):
    z = place[0]
    half = groups // 2

    def take(table, off, src):
        return dot(one_hot(table, z + off, groups, cap), src[...], 1, 0).astype(BF)

    on_m[...] = take(tm, 1, xm)
    on_p[...] = take(tp, groups - 1, xp)
    for i, (table, src) in enumerate(((t0, x0), (tm, xm), (tp, xp))):
        kept[i * cap : (i + 1) * cap, :] = take(table, 0, src)
        kept[(3 + i) * cap : (4 + i) * cap, :] = take(table, half, src)


def pick_on_kernel(groups, cap, place, t0, tm, tp, x0, xm, xp, x_m, x_p, kept, on_m, on_p):
    high = pl.ds(cap, cap)
    on_m[:cap, :] = x_m[...]
    on_p[:cap, :] = x_p[...]
    pick_kernel(
        groups, cap, place, t0, tm, tp, x0, xm, xp, kept, on_m.at[high], on_p.at[high]
    )


def neuron(current, leak):
    v = current
    dv = jnp.ones_like(current)
    total = jnp.zeros_like(current)
    grad = jnp.zeros_like(current)
    for step in range(STEPS):
        if step:
            v = leak * v + current
            dv = leak * dv + 1.0
        t = jnp.tanh((0.5 * SHARPNESS) * (v - 1.0))
        spike = 0.5 * t + 0.5
        dspike = (0.25 * SHARPNESS) * (1.0 - t * t) * dv
        v = v - spike
        dv = dv - dspike
        total = total + spike
        grad = grad + dspike
    return total * (1.0 / STEPS), grad * (1.0 / STEPS)


def forward_kernel(x, up, decay, rates, slope):
    weights = up[...].reshape(x.shape[1], decay.shape[1])
    rates[...], slope[...] = neuron(dot(x[...], weights, 1, 0), decay[...])


def gate_rows(pairs, z, groups, cap, gates):
    for i, (table, off) in enumerate(pairs):
        row = jnp.where(hits(table, z + off, groups, cap), gate_row(table, z + off, groups), 0.0)
        gates[i * cap : (i + 1) * cap, :] = jnp.broadcast_to(
            jnp.sum(row, axis=1, keepdims=True), (cap, 128)
        )


def spread_rows(pairs, z, groups, cap, products, inner):
    for i, (table, off) in enumerate(pairs):
        value = jnp.sum(products[i * cap : (i + 1) * cap, :], axis=1, keepdims=True)
        inner[i : i + 1, :] = jnp.sum(
            jnp.where(hits(table, z + off, groups, cap), value, 0.0), axis=0, keepdims=True
        )


def pull_back(rows, core, r, slope, grad, gates, products, cg, gated, send):
    gate = gates[rows, 0:1]
    both = r * grad
    acc = both[:, :128]
    for k in range(1, both.shape[1] // 128):
        acc = acc + both[:, k * 128 : (k + 1) * 128]
    products[rows, :] += acc
    current = (gate * grad * slope).astype(BF)
    scaled = (gate * r).astype(BF)
    cg[rows, :] = current
    gated[rows, :] = scaled
    send[...] = jnp.where(core == 0, scaled, current)


def backward_kernel(
    groups, cap, place, t0, tm, tp, c, down, down_far, rates_n, slope_n, rates_f, slope_f,
    cg, gated, send_n, send_f, inner, gates, products,
):
    z, core = place[0], place[1]
    half = groups // 2
    step = pl.program_id(0)
    three = 3 * cap
    pairs = ((t0, 0), (tm, 0), (tp, 0), (t0, half), (tm, half), (tp, half))

    @pl.when(step == 0)
    def _():
        products[...] = jnp.zeros_like(products)
        gate_rows(pairs, z, groups, cap, gates)

    far = down_far[...].reshape(c.shape[1], down_far.shape[2])
    for low, send, rates, slope, grad in (
        (0, send_n, rates_n, slope_n, dot(c[:three, :], down[...], 1, 1)),
        (three, send_f, rates_f, slope_f, dot(c[three:, :], far, 1, 0)),
    ):
        rows = slice(low, low + three)
        pull_back(
            rows, core, rates[...], slope[...], grad, gates, products, cg, gated, send
        )

    @pl.when(step == pl.num_programs(0) - 1)
    def _():
        spread_rows(pairs, z, groups, cap, products, inner)


def onward_kernel(
    groups, cap, place, ta, tb, a, b, up, down, decay, cg, gated, send, inner,
    x, c, gates, products,
):
    z, core = place[0], place[1]
    step = pl.program_id(0)
    pairs = ((ta, 0), (tb, 0))

    @pl.when(step == 0)
    def _():
        products[...] = jnp.zeros_like(products)
        gate_rows(pairs, z, groups, cap, gates)
        x[:cap, :], x[cap:, :] = a[:cap, :], b[:cap, :]
        c[:cap, :], c[cap:, :] = a[cap:, :], b[cap:, :]

    rates, slope = neuron(dot(x[...], up[...], 1, 0), decay[...])
    grad = dot(c[...], down[...], 1, 1)
    rows = slice(0, 2 * cap)
    pull_back(rows, core, rates, slope, grad, gates, products, cg, gated, send)

    @pl.when(step == pl.num_programs(0) - 1)
    def _():
        spread_rows(pairs, z, groups, cap, products, inner)


def lay_out(x_first, grid_width, where, grads, o0, o1, o2a, o2b, o3):
    step = pl.program_id(0)
    each = o0.shape[1]
    for k in range(2):
        chip = 2 * step + k
        y, x = chip // grid_width, lax.rem(chip, grid_width)
        main, other = (x, y) if x_first else (y, x)
        away = lax.rem(main - where + grid_width, grid_width)
        value = grads[k * each : (k + 1) * each]
        middle = grid_width // 2
        for distance, target in ((0, o0), (1, o1), (3, o3)):

            @pl.when(away == distance)
            def _(target=target, value=value, other=other):
                target[other] = value

        @pl.when((away == 2) & (other < middle))
        def _(value=value, other=other):
            o2a[other] = value

        @pl.when((away == 2) & (other >= middle))
        def _(value=value, other=other):
            o2b[other - middle] = value


def weight_near_kernel(
    cap, side, place, x, c, a, b, got, got_d, cg, gated, cg_d, gated_d, got_thin, got_thin_d,
    o0, o1, o2a, o2b, o3, wide, thin,
):
    first = place[1] == 0
    three, four, five = 3 * cap, 4 * cap, 5 * cap
    eight = five + three

    @pl.when(pl.program_id(0) == 0)
    def _():
        thin[:three, :] = jnp.where(first, cg[...], gated[...])
        thin[three:five, :] = jnp.where(first, cg_d[...], gated_d[...])
        thin[five:eight, :] = got_thin[...]
        thin[eight:, :] = got_thin_d[...]

    wide[:three, :] = jnp.where(first, x[...], c[...])
    wide[three:four, :] = jnp.where(first, a[:cap, :], a[cap:, :])
    wide[four:five, :] = jnp.where(first, b[:cap, :], b[cap:, :])
    wide[five:eight, :] = got[...]
    wide[eight:, :] = got_d[...]
    grads = dot(wide[...], thin[...], 0, 0).astype(BF)
    lay_out(False, side, place[2], grads, o0, o1, o2a, o2b, o3)


def weight_far_kernel(
    cap, side, place, x, c, got, cg, gated, got_thin, o0, o1, o2a, o2b, o3, wide, thin
):
    first = place[1] == 0
    three = 3 * cap

    @pl.when(pl.program_id(0) == 0)
    def _():
        thin[:three, :] = jnp.where(first, cg[...], gated[...])
        thin[three:, :] = got_thin[...]

    wide[:three, :] = jnp.where(first, x[...], c[...])
    wide[three:, :] = got[...]
    grads = dot(wide[...], thin[...], 0, 0).astype(BF)
    lay_out(True, side, place[3], grads, o0, o1, o2a, o2b, o3)


def in_two(values, shape):
    row = lax.broadcasted_iota(jnp.int32, shape, 0)
    packed = jnp.zeros(shape, F32)
    for k, value in enumerate(values):
        high = value.astype(BF).astype(F32)
        packed = jnp.where(row == k, high, packed)
        packed = jnp.where(row == k + 3, value - high, packed)
    return packed.astype(BF)


def rows_kernel(
    cap, cg, gated, cg_d, gated_d, inner, inner_d, up, down, up_far, down_far,
    out, back, on_a, on_b,
):
    tokens = inner.shape[1]
    two = 2 * cap
    for on, near, far, away in ((on_a, 1, 4, 0), (on_b, 2, 5, 1)):
        on[two:, :] = jnp.zeros((on.shape[0] - two, on.shape[1]), BF)

        @pl.when(pl.program_id(0) == 0)
        def _(on=on, near=near, far=far, away=away):
            values = (
                inner[near : near + 1, :], inner[far : far + 1, :], inner_d[away : away + 1, :]
            )
            on[two:, :tokens] = in_two(values, (on.shape[0] - two, tokens))

    hidden = up.shape[1]
    three, four = 3 * cap, 4 * cap
    uf = up_far[...].reshape(up.shape[0], hidden)
    df = down_far[...].reshape(up.shape[0], hidden)
    near = jnp.concatenate([gated[:three, :], gated_d[...]], axis=0)
    values = dot(near, down[...], 1, 0).astype(BF)
    out[:three, :], on_a[:cap, :], on_b[:cap, :] = values[:three], values[three:four], values[four:]
    out[three:, :] = dot(gated[three:, :], df, 1, 1).astype(BF)
    near = jnp.concatenate([cg[:three, :], cg_d[...]], axis=0)
    values = dot(near, up[...], 1, 1).astype(BF)
    back[:three, :], on_a[cap:two, :], on_b[cap:two, :] = values[:three], values[three:four], values[four:]
    back[three:, :] = dot(cg[three:, :], uf, 1, 1).astype(BF)


def return_kernel(groups, cap, place, tm, tp, rows, got_m, got_p, *rest):
    z = place[0]
    *extras, to_m, to_p = rest
    count = tm.shape[1]
    for extra, to in zip(extras, (to_m, to_p)):
        to[count:, :] = extra[...]
    half = groups // 2

    def put(table, off, values):
        return dot(one_hot(table, z + off, groups, cap), values, 0, 0)

    for table, i, extra, got, to in (
        (tm, 1, 1, got_m, to_m),
        (tp, 2, groups - 1, got_p, to_p),
    ):
        total = put(table, 0, rows[i * cap : (i + 1) * cap, :])
        total += put(table, half, rows[(3 + i) * cap : (4 + i) * cap, :])
        total += put(table, extra, got[...])
        to[:count, :] = total.astype(BF)


def final_kernel(groups, cap, place, t0, rows, a, b, result):
    z = place[0]
    half = groups // 2
    total = dot(one_hot(t0, z, groups, cap), rows[:cap, :], 0, 0)
    total += dot(one_hot(t0, z + half, groups, cap), rows[3 * cap : 4 * cap, :], 0, 0)
    total += a[...].astype(F32) + b[...].astype(F32)
    result[...] = total.astype(BF)


def local(tokens, cotangent, routes, gate_probs, w_up, w_down, decay_rate):
    rows, width = tokens.shape
    hidden = w_up.shape[2]
    groups = lax.axis_size("expert")
    data = lax.axis_size("dp")
    half = groups // 2
    cap = 3 * rows // groups
    z = lax.axis_index("expert")
    dp = lax.axis_index("dp")
    core = dp % 2
    first_core = core == 0
    chips = data // 2
    side = 4
    row, col = dp // (2 * side), (dp // 2) % side
    place = jnp.stack([z, core, row, col]).astype(jnp.int32)
    up, down = w_up[0], w_down[0]

    def over_z(x, step):
        return lax.ppermute(x, "expert", [(i, (i + step) % groups) for i in range(groups)])

    def over_core(x):
        return lax.ppermute(x, "dp", [(i, i ^ 1) for i in range(data)])

    def over_x(x, step):
        return lax.ppermute(
            x,
            "dp",
            [(i, i - 2 * (i // 2 % side) + 2 * ((i // 2 + step) % side)) for i in range(data)],
        )

    def over_y(x, step):
        return lax.ppermute(
            x, "dp", [(i, (i + 2 * side * step) % data) for i in range(data)]
        )

    def after(x, *done):
        return lax.optimization_barrier((x, *done))[0]

    part = width // data
    up_slice = lax.dynamic_slice_in_dim(up, dp * part, part, 0)
    down_slice = lax.dynamic_slice_in_dim(down, dp * part, part, 1).T
    slices = over_z(jnp.concatenate([up_slice, down_slice], axis=0), half)
    gathered = lax.all_gather(slices, "dp", axis=0, tiled=False)
    decay_far = over_z(decay_rate, half)

    ids = lax.broadcasted_iota(jnp.int32, (groups, 1), 0)
    first = routes[:, 0][None, :] == ids
    second = routes[:, 1][None, :] == ids
    named = first | second
    tri = (
        lax.broadcasted_iota(jnp.int32, (rows, rows), 0)
        < lax.broadcasted_iota(jnp.int32, (rows, rows), 1)
    ).astype(BF)
    rank = jnp.where(named, dot(named.astype(BF), tri, 1, 0), -1.0)
    gates = jnp.where(first, gate_probs[:, 0][None, :], 0.0) + jnp.where(
        second, gate_probs[:, 1][None, :], 0.0
    )
    t0 = jnp.concatenate([rank, gates], axis=0)
    tm, tp, ta, tb = over_z(t0, 1), over_z(t0, -1), over_z(t0, 2), over_z(t0, -2)

    tokens = after(tokens, slices)
    tok_m, tok_p = over_z(tokens, 1), over_z(tokens, -1)
    cotangent = after(cotangent, tok_m, tok_p, tm, tp, ta, tb, decay_far)
    cot_m, cot_p = over_z(cotangent, 1), over_z(cotangent, -1)

    table_spec = whole((2 * groups, rows))
    tile = 512
    steps = width // tile

    def cols(n):
        return pl.BlockSpec((n, tile), lambda j: (0, j))

    def picks(kernel, on, extra):
        return call(
            partial(kernel, groups, cap),
            (steps,),
            [scalars()] + [table_spec] * 3 + [cols(rows)] * 3 + extra,
            [cols(6 * cap), cols(on), cols(on)],
            [jax.ShapeDtypeStruct((n, width), BF) for n in (6 * cap, on, on)],
            [],
        )

    x, x_m, x_p = picks(pick_kernel, cap, [])(place, t0, tm, tp, tokens, tok_m, tok_p)

    ff = 256
    ff_steps = hidden // ff

    def ff_cols(n):
        return pl.BlockSpec((n, ff), lambda j: (0, j))

    def far_ff(which):
        return pl.BlockSpec((data, part, ff), lambda j: (0, which, j))

    total = 8 * cap

    def half_rows(i):
        return pl.BlockSpec((3 * cap, width), lambda j: (i, 0))

    def forward(half_index, spec, *args):
        return call(
            forward_kernel,
            (ff_steps,),
            [half_rows(half_index), spec, ff_cols(1)],
            [ff_cols(three)] * 2,
            [jax.ShapeDtypeStruct((three, hidden), F32)] * 2,
            [],
        )(*args)

    three = 3 * cap
    rates_n, slope_n = forward(0, ff_cols(width), x, up, decay_rate)
    rates_f, slope_f = forward(1, far_ff(0), after(x, rates_n), gathered, decay_far)
    c, on_m, on_p = picks(pick_on_kernel, 2 * cap, [cols(cap)] * 2)(
        after(place, rates_f), t0, tm, tp, cotangent, cot_m, cot_p, x_m, x_p
    )
    on_a, on_b = over_z(on_m, 1), over_z(on_p, -1)
    got = over_core(jnp.where(first_core, c, x))

    down_ff = pl.BlockSpec((ff, width), lambda j: (j, 0))
    cg, gated, send_n, send_f, inner = call(
        partial(backward_kernel, groups, cap),
        (ff_steps,),
        [scalars()] + [table_spec] * 3 + [whole((6 * cap, width)), down_ff, far_ff(1)]
        + [ff_cols(three)] * 4,
        [ff_cols(n * cap) for n in (6, 6, 3, 3)] + [whole((6, rows))],
        [jax.ShapeDtypeStruct((n * cap, hidden), BF) for n in (6, 6, 3, 3)]
        + [jax.ShapeDtypeStruct((6, rows), F32)],
        [pltpu.VMEM((6 * cap, 128), F32)] * 2,
    )(place, t0, tm, tp, c, down, gathered, rates_n, slope_n, rates_f, slope_f)
    got_thin_f = over_core(send_f)
    got_thin = over_core(after(send_n, got_thin_f))

    span = 2 * width // chips

    def span_cols(n, i=0):
        return pl.BlockSpec((n, span), lambda j: (i, j))

    def thin_rows(n, i=0):
        return pl.BlockSpec((n, hidden), lambda j: (i, 0))

    each = width // chips
    counts = (side, side, side // 2, side // 2, side)
    laid = [whole((n, each, hidden)) for n in counts]
    laid_shapes = [jax.ShapeDtypeStruct((n, each, hidden), BF) for n in counts]
    far_parts = call(
        partial(weight_far_kernel, cap, side),
        (chips // 2,),
        [scalars()] + [span_cols(three, 1)] * 3 + [thin_rows(three, 1)] * 2 + [thin_rows(three)],
        laid,
        laid_shapes,
        [pltpu.VMEM((6 * cap, span), BF), pltpu.VMEM((6 * cap, hidden), BF)],
    )(place, x, c, got, cg, gated, got_thin_f)
    cg_d, gated_d, send_d, inner_d = call(
        partial(onward_kernel, groups, cap),
        (ff_steps,),
        [scalars()] + [table_spec] * 2 + [whole((2 * cap, width))] * 2
        + [ff_cols(width), down_ff, ff_cols(1)],
        [ff_cols(2 * cap)] * 3 + [whole((2, rows))],
        [jax.ShapeDtypeStruct((2 * cap, hidden), BF)] * 3
        + [jax.ShapeDtypeStruct((2, rows), F32)],
        [pltpu.VMEM((2 * cap, width), BF)] * 2 + [pltpu.VMEM((2 * cap, 128), F32)] * 2,
    )(after(place, far_parts[0]), ta, tb, on_a, on_b, up, down, decay_rate)
    got_thin_d = over_core(send_d)
    far_a, far_b = after((on_a, on_b), cg_d)
    got_d = over_core(
        jnp.concatenate([jnp.where(first_core, v[cap:], v[:cap]) for v in (far_a, far_b)], axis=0)
    )

    middle = side // 2

    def plus(a, b):
        return (a.astype(F32) + b.astype(F32)).astype(BF)

    def first_half(parts, over_first):
        return over_first(parts[2], 1), over_first(parts[3], -1)

    def second_half(parts, got):
        low = ((0, middle), (0, 0), (0, 0))
        high = ((middle, 0), (0, 0), (0, 0))
        o1, o3 = plus(parts[1], jnp.pad(got[0], low)), plus(parts[4], jnp.pad(got[1], high))
        return o1, o3

    def mine(parts, got, at):
        def one(distance):
            i = (at + distance) % side
            picked = (lax.dynamic_index_in_dim(v, i, 0, False) for v in (parts[0], *got))
            return sum(v.astype(F32) for v in picked)

        return one(0), [one(d).astype(BF) for d in (1, 2, 3)]

    def across(values, over_second):
        return [over_second(v, d + 1) for d, v in enumerate(values)]

    far_next = second_half(far_parts, first_half(far_parts, over_x))

    def far_rows(which):
        return pl.BlockSpec((tile // part, part, hidden), lambda j: (j, which, 0))

    up_rows = pl.BlockSpec((tile, hidden), lambda j: (j, 0))
    more = 16
    sent_rows = (6 * cap, 6 * cap, 2 * cap + more, 2 * cap + more)
    out, back, to_a, to_b = call(
        partial(rows_kernel, cap),
        (steps,),
        [whole((6 * cap, hidden))] * 2 + [whole((2 * cap, hidden))] * 2
        + [whole((6, rows)), whole((2, rows)), up_rows, cols(hidden), far_rows(0), far_rows(1)],
        [cols(n) for n in sent_rows],
        [jax.ShapeDtypeStruct((n, width), BF) for n in sent_rows],
        [],
    )(after(cg, far_next), gated, cg_d, gated_d, inner, inner_d, up, down, gathered, gathered)
    got_m, got_p = over_z(to_a, -1), over_z(to_b, 1)
    near_parts = call(
        partial(weight_near_kernel, cap, side),
        (chips // 2,),
        [scalars()] + [span_cols(three)] * 2 + [span_cols(2 * cap)] * 2
        + [span_cols(three), span_cols(2 * cap)]
        + [thin_rows(three)] * 2 + [thin_rows(2 * cap)] * 2 + [thin_rows(three), thin_rows(2 * cap)],
        laid,
        laid_shapes,
        [pltpu.VMEM((10 * cap, span), BF), pltpu.VMEM((10 * cap, hidden), BF)],
    )(
        after(place, out), x, c, on_a, on_b, got, got_d,
        cg, gated, cg_d, gated_d, got_thin, got_thin_d,
    )

    block = jax.ShapeDtypeStruct((rows, width), BF)
    def onward(which):
        return pl.BlockSpec((cap, tile), lambda j: (which, j))

    extra_rows = pl.BlockSpec((more, tile), lambda j: (2 * cap // more, j))

    def returns(which, more):
        return call(
            partial(return_kernel, groups, cap),
            (steps,),
            [scalars()] + [table_spec] * 2 + [cols(6 * cap), onward(which), onward(which)]
            + ([extra_rows] * 2 if more else []),
            [cols(rows + more)] * 2,
            [jax.ShapeDtypeStruct((rows + more, width), BF)] * 2,
            [],
        )

    finals = call(
        partial(final_kernel, groups, cap),
        (steps,),
        [scalars(), table_spec, cols(6 * cap), cols(rows), cols(rows)],
        cols(rows),
        block,
        [],
    )
    out_m, out_p = returns(0, more)(
        place, tm, tp, after(out, near_parts[0]), got_m, got_p, got_m, got_p
    )
    homes = (over_z(out_m, -1), over_z(out_p, 1))
    far_got = after((over_x(far_next[0], 1), over_x(far_next[1], -1)), out_m)
    far_own, far_send = mine(far_parts, far_got, row)
    far_sent = across(far_send, over_y)
    back_m, back_p = returns(1, 0)(
        after(place, out_m, far_send), tm, tp, back, got_m, got_p
    )
    far_sent = after(far_sent, back_m)
    near_next = second_half(near_parts, after(first_half(near_parts, over_y), far_sent))
    near_got = (over_y(near_next[0], 1), over_y(near_next[1], -1))
    sum_far = far_own + sum(v.astype(F32) for v in far_sent)
    back_m, back_p = after((back_m, back_p), sum_far)
    far_home = over_z(sum_far.astype(BF), half)
    near_own, near_send = mine(near_parts, after(near_got, homes, sum_far), col)
    near_sent = across(near_send, over_x)
    layer_out = finals(after(place, near_send), t0, out, *homes)
    sum_near = near_own + sum(v.astype(F32) for v in near_sent)
    weight = sum_near + far_home.astype(F32)
    keep = jnp.where(first_core, weight[:part], weight[part:])
    give = jnp.where(first_core, weight[part:], weight[:part])
    other = over_core(give)
    up_grad = jnp.where(first_core, keep, other)
    down_grad = jnp.where(first_core, other, keep)
    token_grad = finals(after(place, give), t0, back, over_z(back_m, -1), over_z(back_p, 1))
    def rest_of(array, at, k):
        values = array[at:, :rows].astype(F32)
        return values[k] + values[k + 3]

    from_p, from_m = (partial(rest_of, v, 2 * cap) for v in (got_m, got_p))
    past_p, past_m = (partial(rest_of, v, rows) for v in homes)
    table = jnp.stack(
        [inner[0], from_p(0), past_p(2), from_m(1), inner[3], from_p(1), past_m(2), from_m(0)]
    )
    offset = lax.broadcasted_iota(jnp.int32, (groups, 1), 0)

    def gate_of(k):
        hit = ((routes[:, k] - z) % groups)[None, :] == offset
        return jnp.sum(jnp.where(hit, table, 0.0), axis=0)

    gate_grad = jnp.stack([gate_of(0), gate_of(1)], axis=1)
    return (layer_out, token_grad, gate_grad, up_grad[None], down_grad.T[None])


def solution(mesh):
    rows = P(("dp", "expert"), None)
    weights = P("expert", None, None)
    return jax.shard_map(
        local,
        mesh=mesh,
        in_specs=(rows, rows, rows, rows, weights, weights, P("expert", None)),
        out_specs=(rows, rows, rows, P("expert", "dp", None), P("expert", None, "dp")),
        check_vma=False,
    )
```

```python
from functools import partial

import jax
import jax.numpy as jnp
from jax import lax
from jax.experimental import pallas as pl
from jax.experimental.pallas import tpu as pltpu
from jax.sharding import PartitionSpec as P

STEPS = 4
SHARPNESS = 4.0
BF = jnp.bfloat16
F32 = jnp.float32
VMEM_LIMIT = 56 * 1024 * 1024


def dot(a, b, ca, cb):
    return lax.dot_general(a, b, (((ca,), (cb,)), ((), ())), preferred_element_type=F32)


def call(body, grid, in_specs, out_specs, out_shape, scratch):
    return pl.pallas_call(
        body,
        grid=grid,
        in_specs=in_specs,
        out_specs=out_specs,
        out_shape=out_shape,
        scratch_shapes=scratch,
        compiler_params=pltpu.CompilerParams(
            dimension_semantics=("arbitrary",) * len(grid), vmem_limit_bytes=VMEM_LIMIT
        ),
        cost_estimate=pl.CostEstimate(flops=0, bytes_accessed=1 << 16, transcendentals=0),
    )


def whole(shape):
    return pl.BlockSpec(shape, lambda j: (0,) * len(shape))


def scalars():
    return pl.BlockSpec(memory_space=pltpu.SMEM)


def rank_row(table, e, groups):
    return table[pl.ds(lax.rem(e, groups), 1), :]


def gate_row(table, e, groups):
    return table[pl.ds(lax.rem(e, groups) + groups, 1), :]


def hits(table, e, groups, cap):
    slot = lax.broadcasted_iota(jnp.int32, (cap, table.shape[1]), 0).astype(F32)
    return rank_row(table, e, groups) == slot


def one_hot(table, e, groups, cap):
    return jnp.where(hits(table, e, groups, cap), 1.0, 0.0).astype(BF)


def pick_kernel(groups, cap, place, t0, tm, tp, x0, xm, xp, kept, on_m, on_p):
    z = place[0]
    half = groups // 2

    def take(table, off, src):
        return dot(one_hot(table, z + off, groups, cap), src[...], 1, 0).astype(BF)

    on_m[...] = take(tm, 1, xm)
    on_p[...] = take(tp, groups - 1, xp)
    for i, (table, src) in enumerate(((t0, x0), (tm, xm), (tp, xp))):
        kept[i * cap : (i + 1) * cap, :] = take(table, 0, src)
        kept[(3 + i) * cap : (4 + i) * cap, :] = take(table, half, src)


def pick_on_kernel(groups, cap, place, t0, tm, tp, x0, xm, xp, x_m, x_p, kept, on_m, on_p):
    high = pl.ds(cap, cap)
    on_m[:cap, :] = x_m[...]
    on_p[:cap, :] = x_p[...]
    pick_kernel(
        groups, cap, place, t0, tm, tp, x0, xm, xp, kept, on_m.at[high], on_p.at[high]
    )


def neuron(current, leak):
    v = current
    dv = jnp.ones_like(current)
    total = jnp.zeros_like(current)
    grad = jnp.zeros_like(current)
    for step in range(STEPS):
        if step:
            v = leak * v + current
            dv = leak * dv + 1.0
        t = jnp.tanh((0.5 * SHARPNESS) * (v - 1.0))
        spike = 0.5 * t + 0.5
        dspike = (0.25 * SHARPNESS) * (1.0 - t * t) * dv
        v = v - spike
        dv = dv - dspike
        total = total + spike
        grad = grad + dspike
    return total * (1.0 / STEPS), grad * (1.0 / STEPS)


def forward_kernel(x, up, decay, rates, slope):
    weights = up[...].reshape(x.shape[1], decay.shape[1])
    rates[...], slope[...] = neuron(dot(x[...], weights, 1, 0), decay[...])


def gate_rows(pairs, z, groups, cap, gates):
    for i, (table, off) in enumerate(pairs):
        row = jnp.where(hits(table, z + off, groups, cap), gate_row(table, z + off, groups), 0.0)
        gates[i * cap : (i + 1) * cap, :] = jnp.broadcast_to(
            jnp.sum(row, axis=1, keepdims=True), (cap, 128)
        )


def spread_rows(pairs, z, groups, cap, products, inner):
    for i, (table, off) in enumerate(pairs):
        value = jnp.sum(products[i * cap : (i + 1) * cap, :], axis=1, keepdims=True)
        inner[i : i + 1, :] = jnp.sum(
            jnp.where(hits(table, z + off, groups, cap), value, 0.0), axis=0, keepdims=True
        )


def pull_back(rows, core, r, slope, grad, gates, products, cg, gated, send):
    gate = gates[rows, 0:1]
    both = r * grad
    acc = both[:, :128]
    for k in range(1, both.shape[1] // 128):
        acc = acc + both[:, k * 128 : (k + 1) * 128]
    products[rows, :] += acc
    current = (gate * grad * slope).astype(BF)
    scaled = (gate * r).astype(BF)
    cg[rows, :] = current
    gated[rows, :] = scaled
    send[...] = jnp.where(core == 0, scaled, current)


def backward_kernel(
    groups, cap, place, t0, tm, tp, c, down, down_far, rates_n, slope_n, rates_f, slope_f,
    cg, gated, send_n, send_f, inner, gates, products,
):
    z, core = place[0], place[1]
    half = groups // 2
    step = pl.program_id(0)
    three = 3 * cap
    pairs = ((t0, 0), (tm, 0), (tp, 0), (t0, half), (tm, half), (tp, half))

    @pl.when(step == 0)
    def _():
        products[...] = jnp.zeros_like(products)
        gate_rows(pairs, z, groups, cap, gates)

    far = down_far[...].reshape(c.shape[1], down_far.shape[2])
    for low, send, rates, slope, grad in (
        (0, send_n, rates_n, slope_n, dot(c[:three, :], down[...], 1, 1)),
        (three, send_f, rates_f, slope_f, dot(c[three:, :], far, 1, 0)),
    ):
        rows = slice(low, low + three)
        pull_back(
            rows, core, rates[...], slope[...], grad, gates, products, cg, gated, send
        )

    @pl.when(step == pl.num_programs(0) - 1)
    def _():
        spread_rows(pairs, z, groups, cap, products, inner)


def onward_kernel(
    groups, cap, place, ta, tb, a, b, up, down, decay, cg, gated, send, inner,
    x, c, gates, products,
):
    z, core = place[0], place[1]
    step = pl.program_id(0)
    pairs = ((ta, 0), (tb, 0))

    @pl.when(step == 0)
    def _():
        products[...] = jnp.zeros_like(products)
        gate_rows(pairs, z, groups, cap, gates)
        x[:cap, :], x[cap:, :] = a[:cap, :], b[:cap, :]
        c[:cap, :], c[cap:, :] = a[cap:, :], b[cap:, :]

    rates, slope = neuron(dot(x[...], up[...], 1, 0), decay[...])
    grad = dot(c[...], down[...], 1, 1)
    rows = slice(0, 2 * cap)
    pull_back(rows, core, rates, slope, grad, gates, products, cg, gated, send)

    @pl.when(step == pl.num_programs(0) - 1)
    def _():
        spread_rows(pairs, z, groups, cap, products, inner)


def lay_out(x_first, grid_width, where, grads, o0, o1, o2a, o2b, o3):
    step = pl.program_id(0)
    each = o0.shape[1]
    for k in range(2):
        chip = 2 * step + k
        y, x = chip // grid_width, lax.rem(chip, grid_width)
        main, other = (x, y) if x_first else (y, x)
        away = lax.rem(main - where + grid_width, grid_width)
        value = grads[k * each : (k + 1) * each]
        middle = grid_width // 2
        for distance, target in ((0, o0), (1, o1), (3, o3)):

            @pl.when(away == distance)
            def _(target=target, value=value, other=other):
                target[other] = value

        @pl.when((away == 2) & (other < middle))
        def _(value=value, other=other):
            o2a[other] = value

        @pl.when((away == 2) & (other >= middle))
        def _(value=value, other=other):
            o2b[other - middle] = value


def weight_near_kernel(
    cap, side, place, x, c, a, b, got, got_d, cg, gated, cg_d, gated_d, got_thin, got_thin_d,
    o0, o1, o2a, o2b, o3, wide, thin,
):
    first = place[1] == 0
    three, four, five = 3 * cap, 4 * cap, 5 * cap
    eight = five + three

    @pl.when(pl.program_id(0) == 0)
    def _():
        thin[:three, :] = jnp.where(first, cg[...], gated[...])
        thin[three:five, :] = jnp.where(first, cg_d[...], gated_d[...])
        thin[five:eight, :] = got_thin[...]
        thin[eight:, :] = got_thin_d[...]

    wide[:three, :] = jnp.where(first, x[...], c[...])
    wide[three:four, :] = jnp.where(first, a[:cap, :], a[cap:, :])
    wide[four:five, :] = jnp.where(first, b[:cap, :], b[cap:, :])
    wide[five:eight, :] = got[...]
    wide[eight:, :] = got_d[...]
    grads = dot(wide[...], thin[...], 0, 0).astype(BF)
    lay_out(False, side, place[2], grads, o0, o1, o2a, o2b, o3)


def weight_far_kernel(
    cap, side, place, x, c, got, cg, gated, got_thin, o0, o1, o2a, o2b, o3, wide, thin
):
    first = place[1] == 0
    three = 3 * cap

    @pl.when(pl.program_id(0) == 0)
    def _():
        thin[:three, :] = jnp.where(first, cg[...], gated[...])
        thin[three:, :] = got_thin[...]

    wide[:three, :] = jnp.where(first, x[...], c[...])
    wide[three:, :] = got[...]
    grads = dot(wide[...], thin[...], 0, 0).astype(BF)
    lay_out(True, side, place[3], grads, o0, o1, o2a, o2b, o3)


def in_two(values, shape):
    row = lax.broadcasted_iota(jnp.int32, shape, 0)
    packed = jnp.zeros(shape, F32)
    for k, value in enumerate(values):
        high = value.astype(BF).astype(F32)
        packed = jnp.where(row == k, high, packed)
        packed = jnp.where(row == k + 3, value - high, packed)
    return packed.astype(BF)


def rows_kernel(
    cap, cg, gated, cg_d, gated_d, inner, inner_d, up, down, up_far, down_far,
    out, back, on_a, on_b,
):
    tokens = inner.shape[1]
    two = 2 * cap
    for on, near, far, away in ((on_a, 1, 4, 0), (on_b, 2, 5, 1)):
        on[two:, :] = jnp.zeros((on.shape[0] - two, on.shape[1]), BF)

        @pl.when(pl.program_id(0) == 0)
        def _(on=on, near=near, far=far, away=away):
            values = (
                inner[near : near + 1, :], inner[far : far + 1, :], inner_d[away : away + 1, :]
            )
            on[two:, :tokens] = in_two(values, (on.shape[0] - two, tokens))

    hidden = up.shape[1]
    three, four = 3 * cap, 4 * cap
    uf = up_far[...].reshape(up.shape[0], hidden)
    df = down_far[...].reshape(up.shape[0], hidden)
    near = jnp.concatenate([gated[:three, :], gated_d[...]], axis=0)
    values = dot(near, down[...], 1, 0).astype(BF)
    out[:three, :], on_a[:cap, :], on_b[:cap, :] = values[:three], values[three:four], values[four:]
    out[three:, :] = dot(gated[three:, :], df, 1, 1).astype(BF)
    near = jnp.concatenate([cg[:three, :], cg_d[...]], axis=0)
    values = dot(near, up[...], 1, 1).astype(BF)
    back[:three, :], on_a[cap:two, :], on_b[cap:two, :] = values[:three], values[three:four], values[four:]
    back[three:, :] = dot(cg[three:, :], uf, 1, 1).astype(BF)


def return_kernel(groups, cap, place, tm, tp, rows, got_m, got_p, *rest):
    z = place[0]
    *extras, to_m, to_p = rest
    count = tm.shape[1]
    for extra, to in zip(extras, (to_m, to_p)):
        to[count:, :] = extra[...]
    half = groups // 2

    def put(table, off, values):
        return dot(one_hot(table, z + off, groups, cap), values, 0, 0)

    for table, i, extra, got, to in (
        (tm, 1, 1, got_m, to_m),
        (tp, 2, groups - 1, got_p, to_p),
    ):
        total = put(table, 0, rows[i * cap : (i + 1) * cap, :])
        total += put(table, half, rows[(3 + i) * cap : (4 + i) * cap, :])
        total += put(table, extra, got[...])
        to[:count, :] = total.astype(BF)


def final_kernel(groups, cap, place, t0, rows, a, b, result):
    z = place[0]
    half = groups // 2
    total = dot(one_hot(t0, z, groups, cap), rows[:cap, :], 0, 0)
    total += dot(one_hot(t0, z + half, groups, cap), rows[3 * cap : 4 * cap, :], 0, 0)
    total += a[...].astype(F32) + b[...].astype(F32)
    result[...] = total.astype(BF)


def local(tokens, cotangent, routes, gate_probs, w_up, w_down, decay_rate):
    rows, width = tokens.shape
    hidden = w_up.shape[2]
    groups = lax.axis_size("expert")
    data = lax.axis_size("dp")
    half = groups // 2
    cap = 3 * rows // groups
    z = lax.axis_index("expert")
    dp = lax.axis_index("dp")
    core = dp % 2
    first_core = core == 0
    chips = data // 2
    side = 4
    row, col = dp // (2 * side), (dp // 2) % side
    place = jnp.stack([z, core, row, col]).astype(jnp.int32)
    up, down = w_up[0], w_down[0]

    def over_z(x, step):
        return lax.ppermute(x, "expert", [(i, (i + step) % groups) for i in range(groups)])

    def over_core(x):
        return lax.ppermute(x, "dp", [(i, i ^ 1) for i in range(data)])

    def over_x(x, step):
        return lax.ppermute(
            x,
            "dp",
            [(i, i - 2 * (i // 2 % side) + 2 * ((i // 2 + step) % side)) for i in range(data)],
        )

    def over_y(x, step):
        return lax.ppermute(
            x, "dp", [(i, (i + 2 * side * step) % data) for i in range(data)]
        )

    def after(x, *done):
        return lax.optimization_barrier((x, *done))[0]

    part = width // data
    up_slice = lax.dynamic_slice_in_dim(up, dp * part, part, 0)
    down_slice = lax.dynamic_slice_in_dim(down, dp * part, part, 1).T
    slices = over_z(jnp.concatenate([up_slice, down_slice], axis=0), half)
    gathered = lax.all_gather(slices, "dp", axis=0, tiled=False)
    decay_far = over_z(decay_rate, half)

    ids = lax.broadcasted_iota(jnp.int32, (groups, 1), 0)
    first = routes[:, 0][None, :] == ids
    second = routes[:, 1][None, :] == ids
    named = first | second
    tri = (
        lax.broadcasted_iota(jnp.int32, (rows, rows), 0)
        < lax.broadcasted_iota(jnp.int32, (rows, rows), 1)
    ).astype(BF)
    rank = jnp.where(named, dot(named.astype(BF), tri, 1, 0), -1.0)
    gates = jnp.where(first, gate_probs[:, 0][None, :], 0.0) + jnp.where(
        second, gate_probs[:, 1][None, :], 0.0
    )
    t0 = jnp.concatenate([rank, gates], axis=0)
    tm, tp, ta, tb = over_z(t0, 1), over_z(t0, -1), over_z(t0, 2), over_z(t0, -2)

    tokens = after(tokens, slices)
    tok_m, tok_p = over_z(tokens, 1), over_z(tokens, -1)
    cotangent = after(cotangent, tok_m, tok_p, tm, tp, ta, tb, decay_far)
    cot_m, cot_p = over_z(cotangent, 1), over_z(cotangent, -1)

    table_spec = whole((2 * groups, rows))
    tile = 512
    steps = width // tile

    def cols(n):
        return pl.BlockSpec((n, tile), lambda j: (0, j))

    def picks(kernel, on, extra):
        return call(
            partial(kernel, groups, cap),
            (steps,),
            [scalars()] + [table_spec] * 3 + [cols(rows)] * 3 + extra,
            [cols(6 * cap), cols(on), cols(on)],
            [jax.ShapeDtypeStruct((n, width), BF) for n in (6 * cap, on, on)],
            [],
        )

    x, x_m, x_p = picks(pick_kernel, cap, [])(place, t0, tm, tp, tokens, tok_m, tok_p)

    ff = 256
    ff_steps = hidden // ff

    def ff_cols(n):
        return pl.BlockSpec((n, ff), lambda j: (0, j))

    def far_ff(which):
        return pl.BlockSpec((data, part, ff), lambda j: (0, which, j))

    total = 8 * cap

    def half_rows(i):
        return pl.BlockSpec((3 * cap, width), lambda j: (i, 0))

    def forward(half_index, spec, *args):
        return call(
            forward_kernel,
            (ff_steps,),
            [half_rows(half_index), spec, ff_cols(1)],
            [ff_cols(three)] * 2,
            [jax.ShapeDtypeStruct((three, hidden), F32)] * 2,
            [],
        )(*args)

    three = 3 * cap
    rates_n, slope_n = forward(0, ff_cols(width), x, up, decay_rate)
    rates_f, slope_f = forward(1, far_ff(0), after(x, rates_n), gathered, decay_far)
    c, on_m, on_p = picks(pick_on_kernel, 2 * cap, [cols(cap)] * 2)(
        after(place, rates_f), t0, tm, tp, cotangent, cot_m, cot_p, x_m, x_p
    )
    on_a, on_b = over_z(on_m, 1), over_z(on_p, -1)
    got = over_core(jnp.where(first_core, c, x))

    down_ff = pl.BlockSpec((ff, width), lambda j: (j, 0))
    cg, gated, send_n, send_f, inner = call(
        partial(backward_kernel, groups, cap),
        (ff_steps,),
        [scalars()] + [table_spec] * 3 + [whole((6 * cap, width)), down_ff, far_ff(1)]
        + [ff_cols(three)] * 4,
        [ff_cols(n * cap) for n in (6, 6, 3, 3)] + [whole((6, rows))],
        [jax.ShapeDtypeStruct((n * cap, hidden), BF) for n in (6, 6, 3, 3)]
        + [jax.ShapeDtypeStruct((6, rows), F32)],
        [pltpu.VMEM((6 * cap, 128), F32)] * 2,
    )(place, t0, tm, tp, c, down, gathered, rates_n, slope_n, rates_f, slope_f)
    got_thin_f = over_core(send_f)
    got_thin = over_core(after(send_n, got_thin_f))

    span = 2 * width // chips

    def span_cols(n, i=0):
        return pl.BlockSpec((n, span), lambda j: (i, j))

    def thin_rows(n, i=0):
        return pl.BlockSpec((n, hidden), lambda j: (i, 0))

    each = width // chips
    counts = (side, side, side // 2, side // 2, side)
    laid = [whole((n, each, hidden)) for n in counts]
    laid_shapes = [jax.ShapeDtypeStruct((n, each, hidden), BF) for n in counts]
    far_parts = call(
        partial(weight_far_kernel, cap, side),
        (chips // 2,),
        [scalars()] + [span_cols(three, 1)] * 3 + [thin_rows(three, 1)] * 2 + [thin_rows(three)],
        laid,
        laid_shapes,
        [pltpu.VMEM((6 * cap, span), BF), pltpu.VMEM((6 * cap, hidden), BF)],
    )(place, x, c, got, cg, gated, got_thin_f)
    cg_d, gated_d, send_d, inner_d = call(
        partial(onward_kernel, groups, cap),
        (ff_steps,),
        [scalars()] + [table_spec] * 2 + [whole((2 * cap, width))] * 2
        + [ff_cols(width), down_ff, ff_cols(1)],
        [ff_cols(2 * cap)] * 3 + [whole((2, rows))],
        [jax.ShapeDtypeStruct((2 * cap, hidden), BF)] * 3
        + [jax.ShapeDtypeStruct((2, rows), F32)],
        [pltpu.VMEM((2 * cap, width), BF)] * 2 + [pltpu.VMEM((2 * cap, 128), F32)] * 2,
    )(after(place, far_parts[0]), ta, tb, on_a, on_b, up, down, decay_rate)
    got_thin_d = over_core(send_d)
    far_a, far_b = after((on_a, on_b), cg_d)
    got_d = over_core(
        jnp.concatenate([jnp.where(first_core, v[cap:], v[:cap]) for v in (far_a, far_b)], axis=0)
    )

    middle = side // 2

    def plus(a, b):
        return (a.astype(F32) + b.astype(F32)).astype(BF)

    def first_half(parts, over_first):
        return over_first(parts[2], 1), over_first(parts[3], -1)

    def second_half(parts, got):
        low = ((0, middle), (0, 0), (0, 0))
        high = ((middle, 0), (0, 0), (0, 0))
        o1, o3 = plus(parts[1], jnp.pad(got[0], low)), plus(parts[4], jnp.pad(got[1], high))
        return o1, o3

    def mine(parts, got, at):
        def one(distance):
            i = (at + distance) % side
            picked = (lax.dynamic_index_in_dim(v, i, 0, False) for v in (parts[0], *got))
            return sum(v.astype(F32) for v in picked)

        return one(0), [one(d).astype(BF) for d in (1, 2, 3)]

    def across(values, over_second):
        return [over_second(v, d + 1) for d, v in enumerate(values)]

    far_next = second_half(far_parts, first_half(far_parts, over_x))

    def far_rows(which):
        return pl.BlockSpec((tile // part, part, hidden), lambda j: (j, which, 0))

    up_rows = pl.BlockSpec((tile, hidden), lambda j: (j, 0))
    more = 16
    sent_rows = (6 * cap, 6 * cap, 2 * cap + more, 2 * cap + more)
    out, back, to_a, to_b = call(
        partial(rows_kernel, cap),
        (steps,),
        [whole((6 * cap, hidden))] * 2 + [whole((2 * cap, hidden))] * 2
        + [whole((6, rows)), whole((2, rows)), up_rows, cols(hidden), far_rows(0), far_rows(1)],
        [cols(n) for n in sent_rows],
        [jax.ShapeDtypeStruct((n, width), BF) for n in sent_rows],
        [],
    )(after(cg, far_next), gated, cg_d, gated_d, inner, inner_d, up, down, gathered, gathered)
    got_m, got_p = over_z(to_a, -1), over_z(to_b, 1)
    near_parts = call(
        partial(weight_near_kernel, cap, side),
        (chips // 2,),
        [scalars()] + [span_cols(three)] * 2 + [span_cols(2 * cap)] * 2
        + [span_cols(three), span_cols(2 * cap)]
        + [thin_rows(three)] * 2 + [thin_rows(2 * cap)] * 2 + [thin_rows(three), thin_rows(2 * cap)],
        laid,
        laid_shapes,
        [pltpu.VMEM((10 * cap, span), BF), pltpu.VMEM((10 * cap, hidden), BF)],
    )(
        after(place, out), x, c, on_a, on_b, got, got_d,
        cg, gated, cg_d, gated_d, got_thin, got_thin_d,
    )

    block = jax.ShapeDtypeStruct((rows, width), BF)
    def onward(which):
        return pl.BlockSpec((cap, tile), lambda j: (which, j))

    extra_rows = pl.BlockSpec((more, tile), lambda j: (2 * cap // more, j))

    def returns(which, more):
        return call(
            partial(return_kernel, groups, cap),
            (steps,),
            [scalars()] + [table_spec] * 2 + [cols(6 * cap), onward(which), onward(which)]
            + ([extra_rows] * 2 if more else []),
            [cols(rows + more)] * 2,
            [jax.ShapeDtypeStruct((rows + more, width), BF)] * 2,
            [],
        )

    finals = call(
        partial(final_kernel, groups, cap),
        (steps,),
        [scalars(), table_spec, cols(6 * cap), cols(rows), cols(rows)],
        cols(rows),
        block,
        [],
    )
    out_m, out_p = returns(0, more)(
        place, tm, tp, after(out, near_parts[0]), got_m, got_p, got_m, got_p
    )
    homes = (over_z(out_m, -1), over_z(out_p, 1))
    far_got = after((over_x(far_next[0], 1), over_x(far_next[1], -1)), out_m)
    far_send = sum(v.astype(F32) for v in (far_parts[0], *far_got)).astype(BF)
    along_y = [
        [2 * (side * y + x) + c for y in range(side)] for x in range(side) for c in range(2)
    ]
    far_sent = lax.all_to_all(
        far_send, "dp", split_axis=0, concat_axis=0, tiled=True, axis_index_groups=along_y
    )
    near_next = second_half(near_parts, after(first_half(near_parts, over_y), out_m))
    back_m, back_p = returns(1, 0)(
        after(place, out_m, far_send, near_next), tm, tp, back, got_m, got_p
    )
    far_sent = after(far_sent, back_m)
    near_got = (over_y(near_next[0], 1), over_y(near_next[1], -1))
    sum_far = jnp.sum(far_sent.astype(F32), axis=0)
    back_m, back_p = after((back_m, back_p), sum_far)
    far_home = over_z(sum_far.astype(BF), half)
    layer_out = finals(after(place, sum_far), t0, out, *homes)
    near_own, near_send = mine(near_parts, after(near_got, layer_out), col)
    near_sent = across(near_send, over_x)
    sum_near = near_own + sum(v.astype(F32) for v in near_sent)
    weight = sum_near + far_home.astype(F32)
    keep = jnp.where(first_core, weight[:part], weight[part:])
    give = jnp.where(first_core, weight[part:], weight[:part])
    other = over_core(give)
    up_grad = jnp.where(first_core, keep, other)
    down_grad = jnp.where(first_core, other, keep)
    token_grad = finals(after(place, give), t0, back, over_z(back_m, -1), over_z(back_p, 1))
    def rest_of(array, at, k):
        values = array[at:, :rows].astype(F32)
        return values[k] + values[k + 3]

    from_p, from_m = (partial(rest_of, v, 2 * cap) for v in (got_m, got_p))
    past_p, past_m = (partial(rest_of, v, rows) for v in homes)
    table = jnp.stack(
        [inner[0], from_p(0), past_p(2), from_m(1), inner[3], from_p(1), past_m(2), from_m(0)]
    )
    offset = lax.broadcasted_iota(jnp.int32, (groups, 1), 0)

    def gate_of(k):
        hit = ((routes[:, k] - z) % groups)[None, :] == offset
        return jnp.sum(jnp.where(hit, table, 0.0), axis=0)

    gate_grad = jnp.stack([gate_of(0), gate_of(1)], axis=1)
    return (layer_out, token_grad, gate_grad, up_grad[None], down_grad.T[None])


def solution(mesh):
    rows = P(("dp", "expert"), None)
    weights = P("expert", None, None)
    return jax.shard_map(
        local,
        mesh=mesh,
        in_specs=(rows, rows, rows, rows, weights, weights, P("expert", None)),
        out_specs=(rows, rows, rows, P("expert", "dp", None), P("expert", None, "dp")),
        check_vma=False,
    )
```
